256 devices in a mesh: section: 8 (over y, core), expert: 32 (over x, z).
Axes of the slice: x: 4, y: 4, z: 8, core: 2. Of those that a mesh axis runs over, the one named last changes fastest.
Arguments:
- payload_fwd: bfloat16 [8, 4096, 3584], P('section', 'expert'), may hold values from -6 to 6
- scale_fwd: float32 [8, 4096, 28], P('section', 'expert'), may hold values from 0.5 to 2
- routes_fwd: int32 [8, 4096, 1], P('section', 'expert'), may hold values from 0 to 7; in each aligned block of 128 rows (0 to 127, 128 to 255, ..., all dimensions but the last counted through in order) at most 24 rows name the same one
- weight_fwd: float32 [8, 4096, 1], P('section', 'expert'), may hold values from 0.1 to 1
- payload_bwd: bfloat16 [8, 4096, 3584], P('section', 'expert'), may hold values from -6 to 6
- scale_bwd: float32 [8, 4096, 28], P('section', 'expert'), may hold values from 0.5 to 2
- routes_bwd: int32 [8, 4096, 1], P('section', 'expert'), may hold values from 0 to 7; in each aligned block of 128 rows (0 to 127, 128 to 255, ..., all dimensions but the last counted through in order) at most 24 rows name the same one
- weight_bwd: float32 [8, 4096, 1], P('section', 'expert'), may hold values from 0.1 to 1
- cotangent: bfloat16 [8, 4096, 3584], P('section', 'expert'), may hold values from -6 to 6
- norm_gain: float32 [8, 3584], P('section'), may hold values from 0.5 to 2
- gate_proj: bfloat16 [8, 3584, 8192], P('section', None, 'expert'), may hold values from -0.09375 to 0.09375
- up_proj: bfloat16 [8, 3584, 8192], P('section', None, 'expert'), may hold values from -0.09375 to 0.09375
- down_proj: bfloat16 [8, 8192, 3584], P('section', 'expert'), may hold values from -0.1875 to 0.1875
Outputs:
- next_rows: bfloat16 [8, 4096, 3584], P('section', 'expert')
- prev_grads: bfloat16 [8, 4096, 3584], P('section', 'expert')
The draws below stay inside these ranges and needn't reach their ends.
Inputs may be any that keep to these rules, and one draw needn't show every extreme that they name: `routes_fwd`: among the tokens of one device of one layer, no expert is named by more than 24 routes, and in every draw some expert is named by exactly 24. `routes_bwd`: among the tokens of one device of one layer, no expert is named by more than 24 routes, and in every draw some expert is named by exactly 24.
All inputs are finite; a program needn't handle non-finite values.
Results may differ from the reference program's by a relative error of at most 0.0065.
Values may be sent and summed in bfloat16 or wider, within the bound.
No kernel may reach another device: no remote copies, remote signals or barrier semaphores. Data moves between devices by JAX's collectives and lax.ppermute only.
A program may use at most 192 MiB of HBM per device.

```python
import math
import jax
import jax.numpy as jnp
import numpy as np
from jax import lax

D = 3584
FF = 1024
QBLOCK = 128
SPLIT = 4
ROUTES = 1
TOK_DEV = 128
FF_DEV = 256
FLIGHT = 8
TOKENS = 4096
LAYERS = 8
CAP = 24
N_EXPERT = 32


def steps_of(key, dims, split, least, high):
    loudness, own = 1.0, jax.random.fold_in(key, 6)
    for axis_at, shards_of in split:
        draws = jnp.exp(jax.random.uniform(jax.random.fold_in(own, axis_at), (shards_of,), jnp.float32, least / len(split), high / len(split)))
        loudness = loudness * jnp.repeat(draws, dims[axis_at] // shards_of).reshape([-1 if axis == axis_at else 1 for axis in range(len(dims))])
    return loudness


def deal_out(stream_key, own, number, rows, number_of, top, most, slope):
    sequence = jax.random.permutation(stream_key, number_of)
    heavy_load, usual = portions_of(number_of, rows * top, most, slope, True), portions_of(number_of, rows * top, most, slope, False)
    places = jnp.arange(number_of)

    def named(lengths, turn):
        used = int((lengths > 0).sum())
        fixed = max(1, used // 4)
        shifted = fixed + (places - fixed + turn * (used - fixed)) % max(1, number_of - fixed)
        return jnp.zeros((number_of,), jnp.int32).at[sequence[jnp.where(places < fixed, places, shifted)]].set(jnp.asarray(lengths, jnp.int32))

    lengths = jnp.where(number % 4 == 0, named(heavy_load, number // 4), named(usual, number - number // 4 - 1))
    mixed = jax.random.permutation(jax.random.fold_in(own, 3), number_of)
    source_of, receiver = mixed[0:number_of // 2 * 2:2], mixed[1:number_of // 2 * 2:2]
    margin = jnp.minimum(lengths[source_of] - 1, most - lengths[receiver]) // 2
    margin = jnp.where((source_of == sequence[0]) | (receiver == sequence[0]) | (lengths[receiver] == 0), 0, jnp.maximum(margin, 0))
    shifted = jax.random.randint(jax.random.fold_in(own, 4), (number_of // 2,), 0, 1 << 20) % (margin + 1)
    lengths = lengths.at[source_of].add(-shifted).at[receiver].add(shifted)
    labels = jnp.searchsorted(jnp.cumsum(lengths), jnp.arange(rows * top), side="right").astype(jnp.int32)
    table = labels.reshape(top, rows).T
    table = table[jax.random.permutation(jax.random.fold_in(own, 1), rows)]
    turn = jax.random.randint(jax.random.fold_in(own, 2), (rows, 1), 0, top)
    return jnp.take_along_axis(table, (jnp.arange(top)[None, :] + turn) % top, axis=1)


def portions_of(number_of, total, bound, lean, full):
    portions = [(1 << 20) // math.isqrt(grade ** lean) + 1 for grade in range(1, number_of + 1)]
    largest = bound if full else min(bound, max(-(-total // number_of), total * portions[0] // sum(portions)))
    least = 1 if total - largest >= number_of - 1 else 0
    holding, spare = [largest] + [least] * (number_of - 1), total - largest - least * (number_of - 1)
    while spare > 0:
        free = [i for i in range(1, number_of) if holding[i] < largest] or [i for i in range(1, number_of) if holding[i] < bound]
        whole, left = sum([portions[i] for i in free]), spare
        for i in free:
            extra = min(bound - holding[i], max(1, left * portions[i] // whole), spare)
            holding[i] = holding[i] + extra
            spare = spare - extra
    return np.array(holding)


def scatter_about(stream_key, extent, scale, most, cuts=(), held_as=jnp.bfloat16):
    drawn = jax.random.normal(stream_key, extent, jnp.float32) * scale
    if len(cuts) > 0:
        drawn = steps_of(stream_key, extent, cuts, -0.22, 0.18) * drawn
    return jnp.clip(drawn, min=-most, max=most).astype(held_as)


def setup_inputs(seed: int = 0) -> dict:
    key_list = jax.random.split(jax.random.key(seed), 14)
    payload_fwd = scatter_about(key_list[0], (LAYERS, TOKENS, D), 1.0, 6.0, ((0, 8), (1, 32)))
    scale_fwd = jnp.clip(jnp.exp(math.log(2.0) - 1.3862944 * jax.random.uniform(key_list[1], (LAYERS, TOKENS, D // QBLOCK), jnp.float32) ** steps_of(key_list[1], (LAYERS, TOKENS, D // QBLOCK), ((0, 8), (1, 32)), -0.2, 0.2)), 0.5, 2.0)
    routes_fwd_keys = jax.random.split(jax.random.fold_in(key_list[2], 1), LAYERS * TOKENS // TOK_DEV)
    routes_fwd_turns = jax.random.permutation(jax.random.fold_in(key_list[2], 3), LAYERS * TOKENS // TOK_DEV)
    routes_fwd = jax.vmap(lambda own, number: deal_out(jax.random.fold_in(key_list[2], 2), own, number, TOK_DEV, FLIGHT, ROUTES, CAP, 2))(routes_fwd_keys, routes_fwd_turns).reshape((LAYERS, TOKENS, ROUTES))
    weight_fwd = jnp.clip(0.1 + 0.9 * jax.random.uniform(key_list[3], (LAYERS, TOKENS, ROUTES), jnp.float32) ** steps_of(key_list[3], (LAYERS, TOKENS, ROUTES), ((0, 8), (1, 32)), -0.2, 0.2), 0.1, 1.0)
    payload_bwd = scatter_about(key_list[4], (LAYERS, TOKENS, D), 1.0, 6.0, ((0, 8), (1, 32)))
    scale_bwd = jnp.clip(jnp.exp(math.log(2.0) - 1.3862944 * jax.random.uniform(key_list[5], (LAYERS, TOKENS, D // QBLOCK), jnp.float32) ** steps_of(key_list[5], (LAYERS, TOKENS, D // QBLOCK), ((0, 8), (1, 32)), -0.2, 0.2)), 0.5, 2.0)
    routes_bwd_keys = jax.random.split(jax.random.fold_in(key_list[6], 1), LAYERS * TOKENS // TOK_DEV)
    routes_bwd_turns = jax.random.permutation(jax.random.fold_in(key_list[6], 3), LAYERS * TOKENS // TOK_DEV)
    routes_bwd = jax.vmap(lambda own, number: deal_out(jax.random.fold_in(key_list[6], 2), own, number, TOK_DEV, FLIGHT, ROUTES, CAP, 2))(routes_bwd_keys, routes_bwd_turns).reshape((LAYERS, TOKENS, ROUTES))
    weight_bwd = jnp.clip(0.1 + 0.9 * jax.random.uniform(key_list[7], (LAYERS, TOKENS, ROUTES), jnp.float32) ** steps_of(key_list[7], (LAYERS, TOKENS, ROUTES), ((0, 8), (1, 32)), -0.2, 0.2), 0.1, 1.0)
    cotangent = scatter_about(key_list[8], (LAYERS, TOKENS, D), 1.0, 6.0, ((0, 8), (1, 32)))
    norm_gain = jnp.clip(jnp.exp(math.log(2.0) - 1.3862944 * jax.random.uniform(key_list[9], (LAYERS, D), jnp.float32) ** steps_of(key_list[9], (LAYERS, D), ((0, 8),), -0.2, 0.2)), 0.5, 2.0)
    gate_proj = scatter_about(key_list[10], (LAYERS, D, FLIGHT * FF), D ** -0.5, 0.09375, ((0, 8), (2, 32)))
    up_proj = scatter_about(key_list[11], (LAYERS, D, FLIGHT * FF), D ** -0.5, 0.09375, ((0, 8), (2, 32)))
    down_proj = scatter_about(key_list[12], (LAYERS, FLIGHT * FF, D), FF ** -0.5, 0.1875, ((0, 8), (1, 32)))
    return dict(payload_fwd=payload_fwd, scale_fwd=scale_fwd, routes_fwd=routes_fwd, weight_fwd=weight_fwd, payload_bwd=payload_bwd, scale_bwd=scale_bwd, routes_bwd=routes_bwd, weight_bwd=weight_bwd, cotangent=cotangent, norm_gain=norm_gain, gate_proj=gate_proj, up_proj=up_proj, down_proj=down_proj)


EPS = 1e-06

def normed_rows(payload, block_scale, layer_gain):
    row_count, row_width = payload.shape
    blocks = block_scale.shape[1]
    inputs = (payload.astype(jnp.float32).reshape(row_count, blocks, row_width // blocks) * block_scale[:, :, None]).reshape(row_count, row_width)
    inverse = lax.rsqrt(lax.optimization_barrier(jnp.mean(inputs * inputs, axis=1, keepdims=True)) + EPS)
    return (inputs, inverse, (inputs * inverse * layer_gain[None, :]).astype(jnp.bfloat16))

def global_slots(route_ids):
    blocks = route_ids.reshape(N_EXPERT, TOK_DEV * ROUTES)
    onehot = (blocks[:, :, None] == jnp.arange(FLIGHT, dtype=jnp.int32)[None, None, :]).astype(jnp.int32)
    earlier = (jnp.cumsum(onehot, axis=1) - onehot).astype(jnp.int32)
    position = lax.optimization_barrier(jnp.sum(earlier * onehot, axis=2)).astype(jnp.int32)
    source = jnp.arange(N_EXPERT, dtype=jnp.int32)[:, None]
    return (blocks * (N_EXPERT * CAP) + source * CAP + position).astype(jnp.int32).reshape(TOKENS, ROUTES)

def expert_table(slot_ids):
    row_table = jnp.full((FLIGHT * N_EXPERT * CAP,), TOKENS, dtype=jnp.int32)
    owners = jnp.broadcast_to(jnp.arange(TOKENS, dtype=jnp.int32)[:, None], (TOKENS, ROUTES))
    return row_table.at[slot_ids.reshape(-1)].set(owners.reshape(-1)).reshape(FLIGHT, N_EXPERT * CAP)

def padded(row_data):
    return jnp.concatenate([row_data, jnp.zeros((1, row_data.shape[1]), row_data.dtype)], axis=0)

def expert_forward(row_block, gate_part, up_part, down_part):
    summed = jnp.zeros((row_block.shape[0], D), jnp.float32)
    for part_index in range(SPLIT):
        columns = slice(part_index * FF_DEV, (part_index + 1) * FF_DEV)
        gate_value = jnp.dot(row_block, gate_part[:, columns], preferred_element_type=jnp.float32)
        up_value = jnp.dot(row_block, up_part[:, columns], preferred_element_type=jnp.float32)
        hidden = (jax.nn.silu(gate_value) * up_value).astype(jnp.bfloat16)
        partial_out = jnp.dot(hidden, down_part[columns], preferred_element_type=jnp.float32).astype(jnp.bfloat16)
        summed = summed + lax.optimization_barrier(partial_out).astype(jnp.float32)
    return summed.astype(jnp.bfloat16)

def expert_backward(row_block, cot_block, gate_part, up_part, down_part):
    summed = jnp.zeros((row_block.shape[0], D), jnp.float32)
    for part_index in range(SPLIT):
        columns = slice(part_index * FF_DEV, (part_index + 1) * FF_DEV)
        gate_value = jnp.dot(row_block, gate_part[:, columns], preferred_element_type=jnp.float32)
        up_value = jnp.dot(row_block, up_part[:, columns], preferred_element_type=jnp.float32)
        hidden_grad = jnp.dot(cot_block, down_part[columns].T, preferred_element_type=jnp.float32)
        sigmoid_gate = jax.nn.sigmoid(gate_value)
        active = gate_value * sigmoid_gate
        gate_grad = (hidden_grad * up_value * sigmoid_gate * (1.0 + gate_value * (1.0 - sigmoid_gate))).astype(jnp.bfloat16)
        up_grad = (hidden_grad * active).astype(jnp.bfloat16)
        back_part = (jnp.dot(gate_grad, gate_part[:, columns].T, preferred_element_type=jnp.float32) + jnp.dot(up_grad, up_part[:, columns].T, preferred_element_type=jnp.float32)).astype(jnp.bfloat16)
        summed = summed + lax.optimization_barrier(back_part).astype(jnp.float32)
    return summed.astype(jnp.bfloat16)

def reference(payload_fwd, scale_fwd, routes_fwd, weight_fwd, payload_bwd, scale_bwd, routes_bwd, weight_bwd, cotangent, norm_gain, gate_proj, up_proj, down_proj):
    forward_list = []
    backward_list = []
    for layer_index in range(LAYERS):
        gate_layer = gate_proj[layer_index].reshape(D, FLIGHT, FF).transpose(1, 0, 2)
        up_layer = up_proj[layer_index].reshape(D, FLIGHT, FF).transpose(1, 0, 2)
        down_layer = down_proj[layer_index].reshape(FLIGHT, FF, D)
        layer_gain = norm_gain[layer_index]
        inputs, inverse, normed = normed_rows(payload_fwd[layer_index], scale_fwd[layer_index], layer_gain)
        slot_ids = global_slots(routes_fwd[layer_index])
        row_table = expert_table(slot_ids)
        expert_in = padded(normed)[row_table]
        results = lax.map(lambda packed: expert_forward(*packed), (expert_in, gate_layer, up_layer, down_layer))
        picked = results.reshape(-1, D)[slot_ids].astype(jnp.float32)
        mixture = lax.optimization_barrier(jnp.sum(weight_fwd[layer_index][:, :, None] * picked, axis=1))
        forward_list.append((inputs + mixture).astype(jnp.bfloat16))
        inputs, inverse, normed = normed_rows(payload_bwd[layer_index], scale_bwd[layer_index], layer_gain)
        slot_ids = global_slots(routes_bwd[layer_index])
        row_table = expert_table(slot_ids)
        expert_in = padded(normed)[row_table]
        expert_cot = padded(cotangent[layer_index])[row_table]
        results = lax.map(lambda packed: expert_backward(*packed), (expert_in, expert_cot, gate_layer, up_layer, down_layer))
        picked = results.reshape(-1, D)[slot_ids].astype(jnp.float32)
        normed_grad = lax.optimization_barrier(jnp.sum(weight_bwd[layer_index][:, :, None] * picked, axis=1))
        scaled = normed_grad * layer_gain[None, :]
        unit_rows = inputs * inverse
        input_grad = inverse * (scaled - unit_rows * lax.optimization_barrier(jnp.mean(scaled * unit_rows, axis=1, keepdims=True)))
        backward_list.append((cotangent[layer_index].astype(jnp.float32) + input_grad).astype(jnp.bfloat16))
    next_rows = jnp.roll(jnp.stack(forward_list), 1, axis=0)
    prev_grads = jnp.roll(jnp.stack(backward_list), -1, axis=0)
    return (next_rows, prev_grads)
```

```python
import jax
import jax.numpy as jnp
from jax import lax
from jax.sharding import Mesh, PartitionSpec as P

SPLIT = 4
EPS = 1e-06
CONTRACT_LAST = (((1,), (1,)), ((), ()))


def from_behind(value, axis, steps):
    count = lax.axis_size(axis)
    pairs = [(source, (source + steps) % count) for source in range(count)]
    return lax.ppermute(value, axis, pairs)


def normed_rows(payload, block_scale, layer_gain):
    row_count, row_width = payload.shape
    blocks = block_scale.shape[1]
    inputs = (
        payload.astype(jnp.float32).reshape(row_count, blocks, row_width // blocks)
        * block_scale[:, :, None]
    ).reshape(row_count, row_width)
    inverse = lax.rsqrt(jnp.mean(inputs * inputs, axis=1, keepdims=True) + EPS)
    return (inputs, inverse, (inputs * inverse * layer_gain[None, :]).astype(jnp.bfloat16))


def local_slots(route_ids, flight, capacity):
    route = route_ids[:, 0]
    onehot = (route[:, None] == jnp.arange(flight, dtype=jnp.int32)[None, :]).astype(jnp.int32)
    earlier = jnp.cumsum(onehot, axis=0) - onehot
    position = jnp.sum(earlier * onehot, axis=1)
    home = (route % 2) * SPLIT + route // 2
    return home * capacity + position


def pick_matrix(slots, slot_count):
    return (slots[:, None] == jnp.arange(slot_count, dtype=jnp.int32)[None, :]).astype(jnp.bfloat16)


def pack(pick, rows):
    return lax.dot_general(
        pick, rows, (((0,), (0,)), ((), ())), preferred_element_type=jnp.float32
    ).astype(jnp.bfloat16)


def unpack(pick, rows):
    return jnp.dot(pick, rows, preferred_element_type=jnp.float32)


def contract(a, b):
    return lax.dot_general(a, b, CONTRACT_LAST, preferred_element_type=jnp.float32)


def to_expert(rows):
    sent = lax.all_to_all(rows, ("h", "j"), 0, 0, tiled=True)
    return lax.all_gather(sent, "x", tiled=True)


def to_tokens(partial_out):
    summed = lax.psum_scatter(partial_out, "x", scatter_dimension=0, tiled=True)
    return lax.all_to_all(summed, ("h", "j"), 0, 0, tiled=True)


def move_weight(hidden_major):
    spread = lax.all_to_all(hidden_major, "x", 0, 0, tiled=True)
    return lax.all_to_all(spread, "j", 0, 0, tiled=True)


def expert_forward(rows, gate, up, down):
    gate_value = contract(rows, gate)
    up_value = contract(rows, up)
    hidden = (jax.nn.silu(gate_value) * up_value).astype(jnp.bfloat16)
    return jnp.dot(hidden, down, preferred_element_type=jnp.float32).astype(jnp.bfloat16)


def expert_backward(rows, cots, gate, up, down):
    gate_value = contract(rows, gate)
    up_value = contract(rows, up)
    hidden_grad = contract(cots, down)
    sigmoid_gate = jax.nn.sigmoid(gate_value)
    active = gate_value * sigmoid_gate
    gate_grad = (
        hidden_grad * up_value * sigmoid_gate * (1.0 + gate_value * (1.0 - sigmoid_gate))
    ).astype(jnp.bfloat16)
    up_grad = (hidden_grad * active).astype(jnp.bfloat16)
    back = jnp.dot(gate_grad, gate, preferred_element_type=jnp.float32) + jnp.dot(
        up_grad, up, preferred_element_type=jnp.float32
    )
    return back.astype(jnp.bfloat16)


def local(
    payload_fwd,
    scale_fwd,
    routes_fwd,
    weight_fwd,
    payload_bwd,
    scale_bwd,
    routes_bwd,
    weight_bwd,
    cotangent,
    norm_gain,
    gate_proj,
    up_proj,
    down_proj,
):
    layer_gain = norm_gain[0]
    flight = 2 * SPLIT
    token_count = payload_fwd.shape[1]
    capacity = 3 * token_count // (2 * flight)
    slot_count = flight * capacity

    inputs_fwd, _, normed_fwd = normed_rows(payload_fwd[0], scale_fwd[0], layer_gain)
    pick_fwd = pick_matrix(local_slots(routes_fwd[0], flight, capacity), slot_count)
    rows_fwd = to_expert(pack(pick_fwd, normed_fwd))

    inputs_bwd, inverse_bwd, normed_bwd = normed_rows(payload_bwd[0], scale_bwd[0], layer_gain)
    pick_bwd = pick_matrix(local_slots(routes_bwd[0], flight, capacity), slot_count)
    rows_bwd = to_expert(pack(pick_bwd, normed_bwd))
    cots_bwd = to_expert(pack(pick_bwd, cotangent[0]))

    gate = move_weight(gate_proj[0].T)
    up = move_weight(up_proj[0].T)
    down = move_weight(down_proj[0])

    mixed_fwd = to_tokens(expert_forward(rows_fwd, gate, up, down))
    mixed_bwd = to_tokens(expert_backward(rows_bwd, cots_bwd, gate, up, down))

    mixture = weight_fwd[0] * unpack(pick_fwd, mixed_fwd)
    next_value = (inputs_fwd + mixture).astype(jnp.bfloat16)
    next_rows = from_behind(next_value, "section", 1)
    normed_grad = weight_bwd[0] * unpack(pick_bwd, mixed_bwd)
    scaled = normed_grad * layer_gain[None, :]
    unit_rows = inputs_bwd * inverse_bwd
    input_grad = inverse_bwd * (
        scaled - unit_rows * jnp.mean(scaled * unit_rows, axis=1, keepdims=True)
    )
    grad_value = (cotangent[0].astype(jnp.float32) + input_grad).astype(jnp.bfloat16)
    prev_grads = from_behind(grad_value, "section", -1)
    return (next_rows[None], prev_grads[None])


def solution(mesh):
    sections, experts = mesh.devices.shape
    columns = experts // (2 * SPLIT)
    fine = Mesh(mesh.devices.reshape(sections, columns, 2, SPLIT), ("section", "x", "h", "j"))
    expert = ("x", "h", "j")
    rows = P("section", expert, None)
    return jax.shard_map(
        local,
        mesh=fine,
        in_specs=(rows,) * 9
        + (
            P("section", None),
            P("section", None, expert),
            P("section", None, expert),
            P("section", expert, None),
        ),
        out_specs=(rows, rows),
        check_vma=False,
    )
```

```python
import functools

import jax
import jax.numpy as jnp
from jax import lax
from jax.experimental import pallas as pl
from jax.experimental.pallas import tpu as pltpu
from jax.sharding import Mesh, PartitionSpec as P

SPLIT = 4
EPS = 1e-06
CONTRACT_LAST = (((1,), (1,)), ((), ()))
VMEM_BYTES = 48 * 1024 * 1024
CHUNK = 512


def contract(a, b):
    return lax.dot_general(a, b, CONTRACT_LAST, preferred_element_type=jnp.float32)


def mul(a, b):
    return jnp.dot(a, b, preferred_element_type=jnp.float32)


def home_of(route):
    return lax.rem(route, 2) * SPLIT + lax.div(route, 2)


def slots_in_lanes(route_row, route_column, capacity):
    tokens = route_row.shape[1]
    above = lax.broadcasted_iota(jnp.int32, (tokens, tokens), 0)
    here = lax.broadcasted_iota(jnp.int32, (tokens, tokens), 1)
    earlier = jnp.where((route_row == route_column) & (above < here), 1.0, 0.0)
    position = jnp.sum(earlier, axis=0, keepdims=True).astype(jnp.int32)
    return home_of(route_row) * capacity + position


def slots_in_rows(route_row, route_column, capacity):
    tokens = route_row.shape[1]
    here = lax.broadcasted_iota(jnp.int32, (tokens, tokens), 0)
    before = lax.broadcasted_iota(jnp.int32, (tokens, tokens), 1)
    earlier = jnp.where((route_row == route_column) & (before < here), 1.0, 0.0)
    position = jnp.sum(earlier, axis=1, keepdims=True).astype(jnp.int32)
    return home_of(route_column) * capacity + position


def scaled_block(payload_ref, scale_ref, block, width):
    columns = slice(block * width, (block + 1) * width)
    return payload_ref[:, columns].astype(jnp.float32) * scale_ref[:, block : block + 1]


def inverse_of(payload_ref, scale_ref):
    tokens, depth = payload_ref.shape
    blocks = scale_ref.shape[1]
    width = depth // blocks
    total = jnp.zeros((tokens, width), jnp.float32)
    for block in range(blocks):
        value = scaled_block(payload_ref, scale_ref, block, width)
        total = total + value * value
    return lax.rsqrt(jnp.sum(total, axis=1, keepdims=True) * (1.0 / depth) + EPS)


def pack_kernel(capacity, with_cot, *refs):
    if with_cot:
        payload_ref, scale_ref, gain_ref, row_ref, column_ref, cot_ref, out_ref, out_cot_ref = refs
    else:
        payload_ref, scale_ref, gain_ref, row_ref, column_ref, out_ref = refs
    tokens, depth = payload_ref.shape
    blocks = scale_ref.shape[1]
    width = depth // blocks
    slot_count = out_ref.shape[0]
    slots = slots_in_lanes(row_ref[...], column_ref[...], capacity)
    index = lax.broadcasted_iota(jnp.int32, (slot_count, tokens), 0)
    pick = jnp.where(index == slots, 1.0, 0.0).astype(jnp.bfloat16)
    inverse = inverse_of(payload_ref, scale_ref)
    per_chunk = CHUNK // width
    for chunk in range(blocks // per_chunk):
        parts = []
        for block in range(chunk * per_chunk, (chunk + 1) * per_chunk):
            columns = slice(block * width, (block + 1) * width)
            value = scaled_block(payload_ref, scale_ref, block, width)
            parts.append((value * inverse * gain_ref[:, columns]).astype(jnp.bfloat16))
        columns = slice(chunk * CHUNK, (chunk + 1) * CHUNK)
        out_ref[:, columns] = mul(pick, jnp.concatenate(parts, axis=1)).astype(jnp.bfloat16)
        if with_cot:
            out_cot_ref[:, columns] = mul(pick, cot_ref[:, columns]).astype(jnp.bfloat16)


def forward_kernel(rows_ref, pair_ref, down_ref, out_ref):
    hidden_units = down_ref.shape[0]
    both = contract(rows_ref[...], pair_ref[...])
    gate_value, up_value = both[:, :hidden_units], both[:, hidden_units:]
    hidden = (gate_value / (1.0 + jnp.exp(-gate_value)) * up_value).astype(jnp.bfloat16)
    for chunk in range(out_ref.shape[1] // CHUNK):
        columns = slice(chunk * CHUNK, (chunk + 1) * CHUNK)
        out_ref[:, columns] = mul(hidden, down_ref[:, columns]).astype(jnp.bfloat16)


def backward_kernel(rows_ref, cots_ref, pair_ref, down_ref, out_ref):
    hidden_units = down_ref.shape[0]
    both = contract(rows_ref[...], pair_ref[...])
    gate_value, up_value = both[:, :hidden_units], both[:, hidden_units:]
    hidden_grad = contract(cots_ref[...], down_ref[...])
    sigmoid_gate = 1.0 / (1.0 + jnp.exp(-gate_value))
    active = gate_value * sigmoid_gate
    gate_grad = hidden_grad * up_value * sigmoid_gate * (1.0 + gate_value * (1.0 - sigmoid_gate))
    up_grad = hidden_grad * active
    grads = jnp.concatenate([gate_grad, up_grad], axis=1).astype(jnp.bfloat16)
    for chunk in range(out_ref.shape[1] // CHUNK):
        columns = slice(chunk * CHUNK, (chunk + 1) * CHUNK)
        out_ref[:, columns] = mul(grads, pair_ref[:, columns]).astype(jnp.bfloat16)


def pick_rows(row_ref, column_ref, slot_count, capacity):
    slots = slots_in_rows(row_ref[...], column_ref[...], capacity)
    index = lax.broadcasted_iota(jnp.int32, (slots.shape[0], slot_count), 1)
    return jnp.where(index == slots, 1.0, 0.0).astype(jnp.bfloat16)


def next_kernel(capacity, payload_ref, scale_ref, row_ref, column_ref, weight_ref, mixed_ref, out_ref):
    depth = payload_ref.shape[1]
    blocks = scale_ref.shape[1]
    width = depth // blocks
    pick = pick_rows(row_ref, column_ref, mixed_ref.shape[0], capacity)
    per_chunk = CHUNK // width
    for chunk in range(blocks // per_chunk):
        columns = slice(chunk * CHUNK, (chunk + 1) * CHUNK)
        mixture = weight_ref[...] * mul(pick, mixed_ref[:, columns])
        value = jnp.concatenate(
            [
                scaled_block(payload_ref, scale_ref, block, width)
                for block in range(chunk * per_chunk, (chunk + 1) * per_chunk)
            ],
            axis=1,
        )
        out_ref[:, columns] = (value + mixture).astype(jnp.bfloat16)


def prev_kernel(
    capacity,
    payload_ref,
    scale_ref,
    gain_ref,
    row_ref,
    column_ref,
    weight_ref,
    cot_ref,
    mixed_ref,
    out_ref,
    scaled_ref,
):
    tokens, depth = payload_ref.shape
    blocks = scale_ref.shape[1]
    width = depth // blocks
    pick = pick_rows(row_ref, column_ref, mixed_ref.shape[0], capacity)
    inverse = inverse_of(payload_ref, scale_ref)
    total = jnp.zeros((tokens, width), jnp.float32)
    for chunk in range(depth // CHUNK):
        columns = slice(chunk * CHUNK, (chunk + 1) * CHUNK)
        grad = weight_ref[...] * mul(pick, mixed_ref[:, columns])
        scaled_ref[:, columns] = grad * gain_ref[:, columns]
    for block in range(blocks):
        columns = slice(block * width, (block + 1) * width)
        unit = scaled_block(payload_ref, scale_ref, block, width) * inverse
        total = total + scaled_ref[:, columns] * unit
    mean = jnp.sum(total, axis=1, keepdims=True) * (1.0 / depth)
    for block in range(blocks):
        columns = slice(block * width, (block + 1) * width)
        unit = scaled_block(payload_ref, scale_ref, block, width) * inverse
        grad = inverse * (scaled_ref[:, columns] - unit * mean)
        out_ref[:, columns] = (cot_ref[:, columns].astype(jnp.float32) + grad).astype(jnp.bfloat16)


def call(kernel, outs, *args, scratch=(), flops=0):
    traffic = sum(a.size * a.dtype.itemsize for a in args) + sum(2 * r * c for r, c in outs)
    shapes = [jax.ShapeDtypeStruct(shape, jnp.bfloat16) for shape in outs]
    whole = pl.BlockSpec(memory_space=pltpu.VMEM)
    return pl.pallas_call(
        kernel,
        out_shape=shapes if len(outs) > 1 else shapes[0],
        in_specs=[whole] * len(args),
        out_specs=[whole] * len(outs) if len(outs) > 1 else whole,
        scratch_shapes=list(scratch),
        cost_estimate=pl.CostEstimate(flops=flops, bytes_accessed=traffic, transcendentals=0),
        compiler_params=pltpu.CompilerParams(vmem_limit_bytes=VMEM_BYTES),
    )(*args)


def expert_call(kernel, rows, pair, down, flops):
    count, depth = rows[0].shape
    block = count // 4
    block_spec = pl.BlockSpec((block, depth), lambda i: (i, 0))
    traffic = 2 * depth * ((len(rows) + 1) * count + pair.shape[0] + down.shape[0])
    return pl.pallas_call(
        kernel,
        grid=(4,),
        out_shape=jax.ShapeDtypeStruct((count, depth), jnp.bfloat16),
        in_specs=[block_spec] * len(rows)
        + [pl.BlockSpec(pair.shape, lambda i: (0, 0)), pl.BlockSpec(down.shape, lambda i: (0, 0))],
        out_specs=block_spec,
        cost_estimate=pl.CostEstimate(flops=flops, bytes_accessed=traffic, transcendentals=0),
        compiler_params=pltpu.CompilerParams(vmem_limit_bytes=VMEM_BYTES),
    )(*rows, pair, down)


def shifted(value, axis, steps):
    count = lax.axis_size(axis)
    return lax.ppermute(value, axis, [(i, (i + steps) % count) for i in range(count)])


def by_distance(quarters, first):
    return [
        lax.dynamic_index_in_dim(quarters, lax.rem(first + steps, SPLIT), 0, keepdims=False)
        for steps in range(SPLIT)
    ]


def exchange(pieces, axis):
    return [pieces[0]] + [shifted(pieces[steps], axis, steps) for steps in range(1, SPLIT)]


def quarters_of(part):
    return by_distance(part.reshape(SPLIT, -1, part.shape[1]), lax.axis_index("x"))


def regroup(spread):
    by_expert = jnp.stack([spread[0], spread[3], spread[2], spread[1]])
    return by_distance(by_expert, lax.axis_index("j") - lax.axis_index("x") + SPLIT)


def spread_z(rows):
    return lax.all_to_all(rows, ("h", "j"), 0, 0, tiled=True)


def gather_x(rows):
    return lax.all_gather(rows, "x", tiled=True)


def scatter_x(partial_out):
    return lax.psum_scatter(partial_out, "x", scatter_dimension=0, tiled=True)


def local(
    payload_fwd,
    scale_fwd,
    routes_fwd,
    weight_fwd,
    payload_bwd,
    scale_bwd,
    routes_bwd,
    weight_bwd,
    cotangent,
    norm_gain,
    gate_proj,
    up_proj,
    down_proj,
):
    barrier = lax.optimization_barrier
    flight = 2 * SPLIT
    tokens, depth = payload_fwd.shape[1:]
    capacity = 3 * tokens // (2 * flight)
    slot_count = flight * capacity
    packed = (slot_count, depth)
    row_fwd, row_bwd = routes_fwd[0].reshape(1, tokens), routes_bwd[0].reshape(1, tokens)
    cot = cotangent[0]

    down = exchange(quarters_of(down_proj[0]), "x")
    gate, up = quarters_of(gate_proj[0].T), quarters_of(up_proj[0].T)
    packed_fwd = call(
        functools.partial(pack_kernel, capacity, False),
        [packed],
        payload_fwd[0],
        scale_fwd[0],
        norm_gain,
        row_fwd,
        routes_fwd[0],
    )
    down, gate, up, packed_fwd, payload_b = barrier((down, gate, up, packed_fwd, payload_bwd[0]))

    gate, up = exchange(gate, "x"), exchange(up, "x")
    sent_fwd = spread_z(packed_fwd)
    packed_bwd, packed_cot = call(
        functools.partial(pack_kernel, capacity, True),
        [packed, packed],
        payload_b,
        scale_bwd[0],
        norm_gain,
        row_bwd,
        routes_bwd[0],
        cot,
    )
    down = regroup(down)
    gate, up, sent_fwd, packed_bwd, packed_cot, down = barrier(
        (gate, up, sent_fwd, packed_bwd, packed_cot, down)
    )

    rows_fwd = gather_x(sent_fwd)
    down = exchange(down, "j")
    sent_bwd = spread_z(packed_bwd)
    gate, up = regroup(gate), regroup(up)
    down, sent_bwd, gate, up, packed_cot = barrier((down, sent_bwd, gate, up, packed_cot))

    rows_bwd = gather_x(sent_bwd)
    gate = exchange(gate, "j")
    sent_cot = spread_z(packed_cot)
    gate, sent_cot, up = barrier((gate, sent_cot, up))

    cots_bwd = gather_x(sent_cot)
    up = exchange(up, "j")
    pair = jnp.concatenate(gate + up, axis=0)
    down = jnp.concatenate(down, axis=0)

    work = 2 * rows_fwd.size * down.shape[0]
    partial_fwd = expert_call(forward_kernel, [rows_fwd], pair, down, 3 * work)
    partial_bwd = expert_call(backward_kernel, [rows_bwd, cots_bwd], pair, down, 5 * work)
    mixed_fwd = spread_z(scatter_x(partial_fwd))
    mixed_bwd = spread_z(scatter_x(partial_bwd))

    next_value = call(
        functools.partial(next_kernel, capacity),
        [(tokens, depth)],
        payload_fwd[0],
        scale_fwd[0],
        row_fwd,
        routes_fwd[0],
        weight_fwd[0],
        mixed_fwd,
    )
    grad_value = call(
        functools.partial(prev_kernel, capacity),
        [(tokens, depth)],
        payload_bwd[0],
        scale_bwd[0],
        norm_gain,
        row_bwd,
        routes_bwd[0],
        weight_bwd[0],
        cot,
        mixed_bwd,
        scratch=[pltpu.VMEM((tokens, depth), jnp.float32)],
    )
    next_rows = shifted(next_value, "section", 1)
    prev_grads = shifted(grad_value, "section", -1)
    return (next_rows[None], prev_grads[None])


def solution(mesh):
    sections, experts = mesh.devices.shape
    columns = experts // (2 * SPLIT)
    fine = Mesh(mesh.devices.reshape(sections, columns, 2, SPLIT), ("section", "x", "h", "j"))
    expert = ("x", "h", "j")
    rows = P("section", expert, None)
    return jax.shard_map(
        local,
        mesh=fine,
        in_specs=(rows,) * 9
        + (
            P("section", None),
            P("section", None, expert),
            P("section", None, expert),
            P("section", expert, None),
        ),
        out_specs=(rows, rows),
        check_vma=False,
    )
```

```python
import functools

import jax
import jax.numpy as jnp
from jax import lax
from jax.experimental import pallas as pl
from jax.experimental.pallas import tpu as pltpu
from jax.sharding import Mesh, PartitionSpec as P

SPLIT = 4
EPS = 1e-06
CONTRACT_LAST = (((1,), (1,)), ((), ()))
VMEM_BYTES = 48 * 1024 * 1024
CHUNK = 512


def contract(a, b):
    return lax.dot_general(a, b, CONTRACT_LAST, preferred_element_type=jnp.float32)


def mul(a, b):
    return jnp.dot(a, b, preferred_element_type=jnp.float32)


def home_of(route):
    return lax.rem(route, 2) * SPLIT + lax.div(route, 2)


def slots_in_lanes(route_row, route_column, capacity, kinds):
    tokens = route_row.shape[1]
    above = lax.broadcasted_iota(jnp.int32, (tokens, tokens), 0)
    here = lax.broadcasted_iota(jnp.int32, (tokens, tokens), 1)
    earlier = jnp.where((route_row == route_column) & (above < here), 1.0, 0.0)
    position = jnp.sum(earlier, axis=0, keepdims=True).astype(jnp.int32)
    return home_of(route_row) * (kinds * capacity) + position


def slots_in_rows(route_row, route_column, capacity):
    tokens = route_row.shape[1]
    here = lax.broadcasted_iota(jnp.int32, (tokens, tokens), 0)
    before = lax.broadcasted_iota(jnp.int32, (tokens, tokens), 1)
    earlier = jnp.where((route_row == route_column) & (before < here), 1.0, 0.0)
    position = jnp.sum(earlier, axis=1, keepdims=True).astype(jnp.int32)
    return home_of(route_column) * capacity + position


def scaled_block(payload_ref, scale_ref, block, width):
    columns = slice(block * width, (block + 1) * width)
    return payload_ref[:, columns].astype(jnp.float32) * scale_ref[:, block : block + 1]


def inverse_of(payload_ref, scale_ref):
    tokens, depth = payload_ref.shape
    blocks = scale_ref.shape[1]
    width = depth // blocks
    total = jnp.zeros((tokens, width), jnp.float32)
    for block in range(blocks):
        value = scaled_block(payload_ref, scale_ref, block, width)
        total = total + value * value
    return lax.rsqrt(jnp.sum(total, axis=1, keepdims=True) * (1.0 / depth) + EPS)


def pick_slots(row_ref, column_ref, capacity, kinds, kind, count):
    slots = slots_in_lanes(row_ref[...], column_ref[...], capacity, kinds) + kind * capacity
    index = lax.broadcasted_iota(jnp.int32, (count, slots.shape[1]), 0)
    return jnp.where(index == slots, 1.0, 0.0).astype(jnp.bfloat16)


def pack_kernel(capacity, *refs):
    cot_ref, gain_ref, out_ref = refs[-3:]
    count = out_ref.shape[0]
    depth = refs[0].shape[1]
    blocks = refs[1].shape[1]
    width = depth // blocks
    sides = (refs[:4], refs[4:8])
    picks = [
        pick_slots(side[2], side[3], capacity, 3, kind, count)
        for side, kind in ((sides[0], 0), (sides[1], 1), (sides[1], 2))
    ]
    pick = jnp.concatenate(picks, axis=1)
    inverses = [inverse_of(side[0], side[1]) for side in sides]
    per_chunk = CHUNK // width
    for chunk in range(blocks // per_chunk):
        rows = []
        for side, inverse in zip(sides, inverses):
            parts = []
            for block in range(chunk * per_chunk, (chunk + 1) * per_chunk):
                columns = slice(block * width, (block + 1) * width)
                value = scaled_block(side[0], side[1], block, width)
                parts.append((value * inverse * gain_ref[:, columns]).astype(jnp.bfloat16))
            rows.append(jnp.concatenate(parts, axis=1))
        columns = slice(chunk * CHUNK, (chunk + 1) * CHUNK)
        stacked = jnp.concatenate(rows + [cot_ref[:, columns]], axis=0)
        out_ref[:, columns] = mul(pick, stacked).astype(jnp.bfloat16)


def joined(refs):
    return jnp.concatenate([ref[...] for ref in refs], axis=0)


def store_rows(out_refs, hidden, weight_ref):
    depth = weight_ref.shape[1]
    for chunk in range(depth // CHUNK):
        columns = slice(chunk * CHUNK, (chunk + 1) * CHUNK)
        value = mul(hidden, weight_ref[:, columns]).astype(jnp.bfloat16)
        start = 0
        for out_ref in out_refs:
            stop = start + out_ref.shape[0]
            out_ref[:, columns] = value[start:stop]
            start = stop


def forward_kernel(count, *refs):
    row_refs, pair_ref, down_ref, out_refs = refs[:count], refs[count], refs[count + 1], refs[count + 2 :]
    hidden_units = down_ref.shape[0]
    both = contract(joined(row_refs), pair_ref[...])
    gate_value, up_value = both[:, :hidden_units], both[:, hidden_units:]
    hidden = (gate_value / (1.0 + jnp.exp(-gate_value)) * up_value).astype(jnp.bfloat16)
    store_rows(out_refs, hidden, down_ref)


def gate_up_kernel(count, *refs):
    row_refs, pair_ref, out_ref = refs[:count], refs[count], refs[-1]
    out_ref[...] = contract(joined(row_refs), pair_ref[...])


def backward_kernel(count, *refs):
    cot_refs, both_ref, pair_ref, down_ref = refs[:count], *refs[count : count + 3]
    out_refs = refs[count + 3 :]
    hidden_units = down_ref.shape[0]
    gate_value, up_value = both_ref[:, :hidden_units], both_ref[:, hidden_units:]
    hidden_grad = contract(joined(cot_refs), down_ref[...])
    sigmoid_gate = 1.0 / (1.0 + jnp.exp(-gate_value))
    active = gate_value * sigmoid_gate
    gate_grad = hidden_grad * up_value * sigmoid_gate * (1.0 + gate_value * (1.0 - sigmoid_gate))
    up_grad = hidden_grad * active
    grads = jnp.concatenate([gate_grad, up_grad], axis=1).astype(jnp.bfloat16)
    store_rows(out_refs, grads, pair_ref)


def pick_rows(row_ref, column_ref, slot_count, capacity):
    slots = slots_in_rows(row_ref[...], column_ref[...], capacity)
    index = lax.broadcasted_iota(jnp.int32, (slots.shape[0], slot_count), 1)
    return jnp.where(index == slots, 1.0, 0.0).astype(jnp.bfloat16)


def next_kernel(capacity, payload_ref, scale_ref, row_ref, column_ref, weight_ref, mixed_ref, out_ref):
    depth = payload_ref.shape[1]
    blocks = scale_ref.shape[1]
    width = depth // blocks
    pick = pick_rows(row_ref, column_ref, mixed_ref.shape[0], capacity)
    per_chunk = CHUNK // width
    for chunk in range(blocks // per_chunk):
        columns = slice(chunk * CHUNK, (chunk + 1) * CHUNK)
        mixture = weight_ref[...] * mul(pick, mixed_ref[:, columns])
        value = jnp.concatenate(
            [
                scaled_block(payload_ref, scale_ref, block, width)
                for block in range(chunk * per_chunk, (chunk + 1) * per_chunk)
            ],
            axis=1,
        )
        out_ref[:, columns] = (value + mixture).astype(jnp.bfloat16)


def prev_kernel(
    capacity,
    payload_ref,
    scale_ref,
    gain_ref,
    row_ref,
    column_ref,
    weight_ref,
    cot_ref,
    mixed_ref,
    out_ref,
    scaled_ref,
):
    tokens, depth = payload_ref.shape
    blocks = scale_ref.shape[1]
    width = depth // blocks
    pick = pick_rows(row_ref, column_ref, mixed_ref.shape[0], capacity)
    inverse = inverse_of(payload_ref, scale_ref)
    total = jnp.zeros((tokens, width), jnp.float32)
    for chunk in range(depth // CHUNK):
        columns = slice(chunk * CHUNK, (chunk + 1) * CHUNK)
        grad = weight_ref[...] * mul(pick, mixed_ref[:, columns])
        scaled_ref[:, columns] = grad * gain_ref[:, columns]
    for block in range(blocks):
        columns = slice(block * width, (block + 1) * width)
        unit = scaled_block(payload_ref, scale_ref, block, width) * inverse
        total = total + scaled_ref[:, columns] * unit
    mean = jnp.sum(total, axis=1, keepdims=True) * (1.0 / depth)
    for block in range(blocks):
        columns = slice(block * width, (block + 1) * width)
        unit = scaled_block(payload_ref, scale_ref, block, width) * inverse
        grad = inverse * (scaled_ref[:, columns] - unit * mean)
        out_ref[:, columns] = (cot_ref[:, columns].astype(jnp.float32) + grad).astype(jnp.bfloat16)


def call(kernel, outs, *args, scratch=(), flops=0):
    traffic = sum(a.size * a.dtype.itemsize for a in args) + sum(2 * r * c for r, c in outs)
    shapes = [jax.ShapeDtypeStruct(shape, jnp.bfloat16) for shape in outs]
    whole = pl.BlockSpec(memory_space=pltpu.VMEM)
    return pl.pallas_call(
        kernel,
        out_shape=shapes if len(outs) > 1 else shapes[0],
        in_specs=[whole] * len(args),
        out_specs=[whole] * len(outs) if len(outs) > 1 else whole,
        scratch_shapes=list(scratch),
        cost_estimate=pl.CostEstimate(flops=flops, bytes_accessed=traffic, transcendentals=0),
        compiler_params=pltpu.CompilerParams(vmem_limit_bytes=VMEM_BYTES),
    )(*args)


def expert_call(kernel, blocks, whole, outs):
    specs = [
        pl.BlockSpec((rows, array.shape[1]), lambda i, at=at: (at, 0)) for array, rows, at in blocks
    ] + [pl.BlockSpec(array.shape, lambda i: (0, 0)) for array in whole]
    return pl.pallas_call(
        kernel,
        grid=(1,),
        out_shape=outs,
        in_specs=specs,
        out_specs=[pl.BlockSpec(out.shape, lambda i: (0, 0)) for out in outs],
        compiler_params=pltpu.CompilerParams(vmem_limit_bytes=VMEM_BYTES),
    )(*[array for array, _, _ in blocks], *whole)


def shifted(value, axis, steps):
    count = lax.axis_size(axis)
    return lax.ppermute(value, axis, [(i, (i + steps) % count) for i in range(count)])


def by_distance(quarters, first):
    return [
        lax.dynamic_index_in_dim(quarters, lax.rem(first + steps, SPLIT), 0, keepdims=False)
        for steps in range(SPLIT)
    ]


def exchange(pieces, axis):
    return [pieces[0]] + [shifted(pieces[steps], axis, steps) for steps in range(1, SPLIT)]


def quarters_of(parts):
    quarters = [part.reshape(SPLIT, -1, part.shape[1]) for part in parts]
    whole = quarters[0] if len(quarters) == 1 else jnp.concatenate(quarters, axis=1)
    return by_distance(whole, lax.axis_index("x"))


def regroup(spread):
    by_expert = jnp.stack([spread[0], spread[3], spread[2], spread[1]])
    return by_distance(by_expert, lax.axis_index("j") - lax.axis_index("x") + SPLIT)


def join(pieces):
    rows = pieces[0].shape[0] // 3
    pair = [p[:rows] for p in pieces] + [p[rows : 2 * rows] for p in pieces]
    down = [p[2 * rows :] for p in pieces]
    return jnp.concatenate(pair, axis=0), jnp.concatenate(down, axis=0)


def spread_z(rows):
    return lax.all_to_all(rows, ("h", "j"), 0, 0, tiled=True)


def both_ways(ahead, behind):
    return shifted(ahead, "x", 1), shifted(behind, "x", -1)


def add(*terms):
    total = terms[0].astype(jnp.float32)
    for term in terms[1:]:
        total = total + term.astype(jnp.float32)
    return total.astype(jnp.bfloat16)


def with_far(ahead, behind, from_left, from_right):
    half = from_left.shape[0]
    ahead = jnp.concatenate([add(ahead[:half], from_left), ahead[half:]], axis=0)
    behind = jnp.concatenate([behind[:half], add(behind[half:], from_right)], axis=0)
    return ahead, behind


def local(
    payload_fwd,
    scale_fwd,
    routes_fwd,
    weight_fwd,
    payload_bwd,
    scale_bwd,
    routes_bwd,
    weight_bwd,
    cotangent,
    norm_gain,
    gate_proj,
    up_proj,
    down_proj,
):
    barrier = lax.optimization_barrier
    flight = 2 * SPLIT
    tokens, depth = payload_fwd.shape[1:]
    capacity = 3 * tokens // (2 * flight)
    slot_count = flight * capacity
    row_fwd, row_bwd = routes_fwd[0].reshape(1, tokens), routes_bwd[0].reshape(1, tokens)
    cot = cotangent[0]
    n, half = slot_count, slot_count // 2

    def row_block(rows):
        return jax.ShapeDtypeStruct((rows, depth), jnp.bfloat16)

    packed = call(
        functools.partial(pack_kernel, capacity),
        [(3 * n, depth)],
        payload_fwd[0],
        scale_fwd[0],
        row_fwd,
        routes_fwd[0],
        payload_bwd[0],
        scale_bwd[0],
        row_bwd,
        routes_bwd[0],
        cot,
        norm_gain,
    )
    sent = spread_z(packed).reshape(flight, 3, capacity, depth)
    sent = sent.transpose(1, 0, 2, 3).reshape(3 * n, depth)
    down = exchange(quarters_of([down_proj[0]]), "x")
    pair = exchange(quarters_of([gate_proj[0].T, up_proj[0].T]), "x")
    weights = regroup([jnp.concatenate([p, d], axis=0) for p, d in zip(pair, down)])
    sent, weights = barrier((sent, weights))

    weights = exchange(weights, "j")
    left, right = barrier(both_ways(sent, sent))
    far_f, far_v = both_ways(left[:n], right[n : 2 * n])
    weights, far_f, far_v, left, right = barrier((weights, far_f, far_v, left, right))

    top_c, bottom_c = both_ways(left[2 * n : 2 * n + half], right[2 * n + half :])
    pair, down = join(weights)
    far_top, far_bottom, own_f, behind_f, ahead_f = expert_call(
        functools.partial(forward_kernel, 4),
        [(far_f, n, 0), (sent, n, 0), (left, n, 0), (right, n, 0)],
        [pair, down],
        [row_block(rows) for rows in (half, half, n, n, n)],
    )
    top_c, bottom_c, far_top, far_bottom = barrier((top_c, bottom_c, far_top, far_bottom))

    back_f = both_ways(far_top, far_bottom)
    (both,) = expert_call(
        functools.partial(gate_up_kernel, 4),
        [(far_v, n, 0), (sent, n, 1), (left, n, 1), (right, n, 1)],
        [pair],
        [jax.ShapeDtypeStruct((SPLIT * n, pair.shape[0]), jnp.float32)],
    )
    back_f, both = barrier((back_f, both))

    back_f = both_ways(*with_far(ahead_f, behind_f, *back_f))
    far_top, far_bottom, own_b, behind_b, ahead_b = expert_call(
        functools.partial(backward_kernel, 5),
        [(top_c, half, 0), (bottom_c, half, 0), (sent, n, 2), (left, n, 2), (right, n, 2)],
        [both, pair, down],
        [row_block(rows) for rows in (half, half, n, n, n)],
    )
    back_f, far_top, far_bottom = barrier((back_f, far_top, far_bottom))

    mixed_fwd = spread_z(add(own_f, *back_f))
    back_b = barrier(both_ways(far_top, far_bottom))
    back_b = both_ways(*with_far(ahead_b, behind_b, *back_b))
    back_b, mixed_fwd = barrier((back_b, mixed_fwd))
    mixed_bwd = spread_z(add(own_b, *back_b))

    next_value = call(
        functools.partial(next_kernel, capacity),
        [(tokens, depth)],
        payload_fwd[0],
        scale_fwd[0],
        row_fwd,
        routes_fwd[0],
        weight_fwd[0],
        mixed_fwd,
    )
    grad_value = call(
        functools.partial(prev_kernel, capacity),
        [(tokens, depth)],
        payload_bwd[0],
        scale_bwd[0],
        norm_gain,
        row_bwd,
        routes_bwd[0],
        weight_bwd[0],
        cot,
        mixed_bwd,
        scratch=[pltpu.VMEM((tokens, depth), jnp.float32)],
    )
    next_rows = shifted(next_value, "section", 1)
    prev_grads = shifted(grad_value, "section", -1)
    return (next_rows[None], prev_grads[None])


def solution(mesh):
    sections, experts = mesh.devices.shape
    columns = experts // (2 * SPLIT)
    fine = Mesh(mesh.devices.reshape(sections, columns, 2, SPLIT), ("section", "x", "h", "j"))
    expert = ("x", "h", "j")
    rows = P("section", expert, None)
    return jax.shard_map(
        local,
        mesh=fine,
        in_specs=(rows,) * 9
        + (
            P("section", None),
            P("section", None, expert),
            P("section", None, expert),
            P("section", expert, None),
        ),
        out_specs=(rows, rows),
        check_vma=False,
    )
```

```python
import functools

import jax
import jax.numpy as jnp
from jax import lax
from jax.experimental import pallas as pl
from jax.experimental.pallas import tpu as pltpu
from jax.sharding import Mesh, PartitionSpec as P

SPLIT = 4
EPS = 1e-06
CONTRACT_LAST = (((1,), (1,)), ((), ()))
VMEM_BYTES = 48 * 1024 * 1024
ALL_VMEM_BYTES = 60 * 1024 * 1024
CHUNK = 512


def contract(a, b):
    return lax.dot_general(a, b, CONTRACT_LAST, preferred_element_type=jnp.float32)


def mul(a, b):
    return jnp.dot(a, b, preferred_element_type=jnp.float32)


def home_of(route):
    return lax.rem(route, 2) * SPLIT + lax.div(route, 2)


def earlier_of(route_row):
    tokens = route_row.shape[1]
    first = lax.broadcasted_iota(jnp.int32, (tokens, tokens), 0)
    second = lax.broadcasted_iota(jnp.int32, (tokens, tokens), 1)
    column = jnp.sum(jnp.where(first == second, route_row, 0), axis=1, keepdims=True)
    return column, column == route_row, first, second


def slots_in_lanes(route_row, capacity, kinds):
    _, same, above, here = earlier_of(route_row)
    earlier = jnp.where(same & (above < here), 1.0, 0.0)
    position = jnp.sum(earlier, axis=0, keepdims=True).astype(jnp.int32)
    return home_of(route_row) * (kinds * capacity) + position


def slots_in_rows(route_row, capacity):
    column, same, here, before = earlier_of(route_row)
    earlier = jnp.where(same & (before < here), 1.0, 0.0)
    position = jnp.sum(earlier, axis=1, keepdims=True).astype(jnp.int32)
    return home_of(column) * capacity + position


def as_column(row):
    tokens = row.shape[1]
    first = lax.broadcasted_iota(jnp.int32, (tokens, tokens), 0)
    second = lax.broadcasted_iota(jnp.int32, (tokens, tokens), 1)
    return jnp.sum(jnp.where(first == second, row, 0.0), axis=1, keepdims=True)


def scale_columns(scale_ref):
    blocks, _, tokens = scale_ref.shape
    rows = [scale_ref[block] for block in range(blocks)]
    rows.append(jnp.zeros((tokens - blocks, tokens), jnp.float32))
    return jnp.transpose(jnp.concatenate(rows, axis=0))


def scaled_block(payload_ref, scales, block, width):
    columns = slice(block * width, (block + 1) * width)
    return payload_ref[:, columns].astype(jnp.float32) * scales[:, block : block + 1]


def inverse_of(payload_ref, scales, blocks):
    tokens, depth = payload_ref.shape
    width = depth // blocks
    total = jnp.zeros((tokens, width), jnp.float32)
    for block in range(blocks):
        value = scaled_block(payload_ref, scales, block, width)
        total = total + value * value
    return lax.rsqrt(jnp.sum(total, axis=1, keepdims=True) * (1.0 / depth) + EPS)


def pick_slots(row_ref, capacity, kinds, kind, count):
    slots = slots_in_lanes(row_ref[...], capacity, kinds) + kind * capacity
    index = lax.broadcasted_iota(jnp.int32, (count, slots.shape[1]), 0)
    return jnp.where(index == slots, 1.0, 0.0).astype(jnp.bfloat16)


def pack_kernel(capacity, *refs):
    cot_ref, gain_ref, out_ref = refs[-3:]
    count = out_ref.shape[0]
    depth = refs[0].shape[1]
    blocks = refs[1].shape[0]
    width = depth // blocks
    sides = [(refs[at], scale_columns(refs[at + 1]), refs[at + 2]) for at in (0, 3)]
    picks = [
        pick_slots(sides[side][2], capacity, 3, kind, count)
        for side, kind in ((0, 0), (1, 1), (1, 2))
    ]
    pick = jnp.concatenate(picks, axis=1)
    inverses = [inverse_of(side[0], side[1], blocks) for side in sides]
    per_chunk = CHUNK // width
    for chunk in range(blocks // per_chunk):
        rows = []
        for side, inverse in zip(sides, inverses):
            parts = []
            for block in range(chunk * per_chunk, (chunk + 1) * per_chunk):
                columns = slice(block * width, (block + 1) * width)
                value = scaled_block(side[0], side[1], block, width)
                parts.append((value * inverse * gain_ref[:, columns]).astype(jnp.bfloat16))
            rows.append(jnp.concatenate(parts, axis=1))
        columns = slice(chunk * CHUNK, (chunk + 1) * CHUNK)
        stacked = jnp.concatenate(rows + [cot_ref[:, columns]], axis=0)
        out_ref[:, columns] = mul(pick, stacked).astype(jnp.bfloat16)


def joined(refs):
    return jnp.concatenate([ref[...] for ref in refs], axis=0)


def store_rows(out_refs, hidden, weight_ref):
    depth = weight_ref.shape[1]
    for chunk in range(depth // CHUNK):
        columns = slice(chunk * CHUNK, (chunk + 1) * CHUNK)
        value = mul(hidden, weight_ref[:, columns]).astype(jnp.bfloat16)
        start = 0
        for out_ref in out_refs:
            stop = start + out_ref.shape[0]
            out_ref[:, columns] = value[start:stop]
            start = stop


def forward_kernel(count, *refs):
    row_refs, pair_ref, down_ref, out_refs = refs[:count], refs[count], refs[count + 1], refs[count + 2 :]
    hidden_units = down_ref.shape[0]
    both = contract(joined(row_refs), pair_ref[...])
    gate_value, up_value = both[:, :hidden_units], both[:, hidden_units:]
    hidden = (gate_value / (1.0 + jnp.exp(-gate_value)) * up_value).astype(jnp.bfloat16)
    store_rows(out_refs, hidden, down_ref)


def gate_up_kernel(count, *refs):
    row_refs, pair_ref, out_ref = refs[:count], refs[count], refs[-1]
    out_ref[...] = contract(joined(row_refs), pair_ref[...])


def backward_kernel(count, *refs):
    cot_refs, both_ref, pair_ref, down_ref = refs[:count], *refs[count : count + 3]
    out_refs = refs[count + 3 :]
    hidden_units = down_ref.shape[0]
    gate_value, up_value = both_ref[:, :hidden_units], both_ref[:, hidden_units:]
    hidden_grad = contract(joined(cot_refs), down_ref[...])
    sigmoid_gate = 1.0 / (1.0 + jnp.exp(-gate_value))
    active = gate_value * sigmoid_gate
    gate_grad = hidden_grad * up_value * sigmoid_gate * (1.0 + gate_value * (1.0 - sigmoid_gate))
    up_grad = hidden_grad * active
    grads = jnp.concatenate([gate_grad, up_grad], axis=1).astype(jnp.bfloat16)
    store_rows(out_refs, grads, pair_ref)


def pick_rows(row_ref, slot_count, capacity):
    slots = slots_in_rows(row_ref[...], capacity)
    index = lax.broadcasted_iota(jnp.int32, (slots.shape[0], slot_count), 1)
    return jnp.where(index == slots, 1.0, 0.0).astype(jnp.bfloat16)


def next_kernel(capacity, payload_ref, scale_ref, row_ref, weight_ref, mixed_ref, out_ref):
    depth = payload_ref.shape[1]
    blocks = scale_ref.shape[0]
    width = depth // blocks
    scales = scale_columns(scale_ref)
    weight = as_column(weight_ref[...])
    pick = pick_rows(row_ref, mixed_ref.shape[0], capacity)
    per_chunk = CHUNK // width
    for chunk in range(blocks // per_chunk):
        columns = slice(chunk * CHUNK, (chunk + 1) * CHUNK)
        mixture = weight * mul(pick, mixed_ref[:, columns])
        value = jnp.concatenate(
            [
                scaled_block(payload_ref, scales, block, width)
                for block in range(chunk * per_chunk, (chunk + 1) * per_chunk)
            ],
            axis=1,
        )
        out_ref[:, columns] = (value + mixture).astype(jnp.bfloat16)


def prev_kernel(
    capacity,
    payload_ref,
    scale_ref,
    gain_ref,
    row_ref,
    weight_ref,
    cot_ref,
    mixed_ref,
    out_ref,
    scaled_ref,
):
    tokens, depth = payload_ref.shape
    blocks = scale_ref.shape[0]
    width = depth // blocks
    scales = scale_columns(scale_ref)
    weight = as_column(weight_ref[...])
    pick = pick_rows(row_ref, mixed_ref.shape[0], capacity)
    inverse = inverse_of(payload_ref, scales, blocks)
    total = jnp.zeros((tokens, width), jnp.float32)
    for chunk in range(depth // CHUNK):
        columns = slice(chunk * CHUNK, (chunk + 1) * CHUNK)
        grad = weight * mul(pick, mixed_ref[:, columns])
        scaled_ref[:, columns] = grad * gain_ref[:, columns]
    for block in range(blocks):
        columns = slice(block * width, (block + 1) * width)
        unit = scaled_block(payload_ref, scales, block, width) * inverse
        total = total + scaled_ref[:, columns] * unit
    mean = jnp.sum(total, axis=1, keepdims=True) * (1.0 / depth)
    for block in range(blocks):
        columns = slice(block * width, (block + 1) * width)
        unit = scaled_block(payload_ref, scales, block, width) * inverse
        grad = inverse * (scaled_ref[:, columns] - unit * mean)
        out_ref[:, columns] = (cot_ref[:, columns].astype(jnp.float32) + grad).astype(jnp.bfloat16)


def call(kernel, out, *args, scratch=(), vmem=VMEM_BYTES):
    def whole(shape):
        return pl.BlockSpec(shape, lambda i: (0,) * len(shape))

    return pl.pallas_call(
        kernel,
        grid=(1,),
        out_shape=jax.ShapeDtypeStruct(out, jnp.bfloat16),
        in_specs=[whole(arg.shape) for arg in args],
        out_specs=whole(out),
        scratch_shapes=list(scratch),
        compiler_params=pltpu.CompilerParams(vmem_limit_bytes=vmem),
    )(*args)


def expert_call(kernel, blocks, whole, outs):
    specs = [
        pl.BlockSpec((rows, array.shape[1]), lambda i, at=at: (at, 0)) for array, rows, at in blocks
    ] + [pl.BlockSpec(array.shape, lambda i: (0, 0)) for array in whole]
    return pl.pallas_call(
        kernel,
        grid=(1,),
        out_shape=outs,
        in_specs=specs,
        out_specs=[pl.BlockSpec(out.shape, lambda i: (0, 0)) for out in outs],
        compiler_params=pltpu.CompilerParams(vmem_limit_bytes=VMEM_BYTES),
    )(*[array for array, _, _ in blocks], *whole)


def shifted(value, axis, steps):
    count = lax.axis_size(axis)
    return lax.ppermute(value, axis, [(i, (i + steps) % count) for i in range(count)])


def by_distance(quarters, first):
    return [
        lax.dynamic_index_in_dim(quarters, lax.rem(first + steps, SPLIT), 0, keepdims=False)
        for steps in range(SPLIT)
    ]


def exchange(pieces, axis):
    return [pieces[0]] + [shifted(pieces[steps], axis, steps) for steps in range(1, SPLIT)]


def quarters_of(parts):
    quarters = [part.reshape(SPLIT, -1, part.shape[1]) for part in parts]
    whole = quarters[0] if len(quarters) == 1 else jnp.concatenate(quarters, axis=1)
    return by_distance(whole, lax.axis_index("x"))


def regroup(spread):
    by_expert = jnp.stack([spread[0], spread[3], spread[2], spread[1]])
    return by_distance(by_expert, lax.axis_index("j") - lax.axis_index("x") + SPLIT)


def join(pieces):
    rows = pieces[0].shape[0] // 3
    pair = [p[:rows] for p in pieces] + [p[rows : 2 * rows] for p in pieces]
    down = [p[2 * rows :] for p in pieces]
    return jnp.concatenate(pair, axis=0), jnp.concatenate(down, axis=0)


def spread_z(rows):
    return lax.all_to_all(rows, ("h", "j"), 0, 0, tiled=True)


def both_ways(ahead, behind):
    return shifted(ahead, "x", 1), shifted(behind, "x", -1)


def add(*terms):
    total = terms[0].astype(jnp.float32)
    for term in terms[1:]:
        total = total + term.astype(jnp.float32)
    return total.astype(jnp.bfloat16)


def with_far(ahead, behind, from_left, from_right):
    half = from_left.shape[0]
    ahead = jnp.concatenate([add(ahead[:half], from_left), ahead[half:]], axis=0)
    behind = jnp.concatenate([behind[:half], add(behind[half:], from_right)], axis=0)
    return ahead, behind


def local(
    payload_fwd,
    scale_fwd,
    routes_fwd,
    weight_fwd,
    payload_bwd,
    scale_bwd,
    routes_bwd,
    weight_bwd,
    cotangent,
    norm_gain,
    gate_proj,
    up_proj,
    down_proj,
):
    barrier = lax.optimization_barrier
    flight = 2 * SPLIT
    tokens, depth = payload_fwd.shape[1:]
    capacity = 3 * tokens // (2 * flight)
    slot_count = flight * capacity
    row_fwd, row_bwd = routes_fwd[0].reshape(1, tokens), routes_bwd[0].reshape(1, tokens)
    lane_weight_fwd = weight_fwd[0].reshape(1, tokens)
    lane_weight_bwd = weight_bwd[0].reshape(1, tokens)
    lane_scale_fwd = scale_fwd[0].T[:, None, :]
    lane_scale_bwd = scale_bwd[0].T[:, None, :]
    cot = cotangent[0]
    n, half = slot_count, slot_count // 2

    def row_block(rows):
        return jax.ShapeDtypeStruct((rows, depth), jnp.bfloat16)

    packed = call(
        functools.partial(pack_kernel, capacity),
        (3 * n, depth),
        payload_fwd[0],
        lane_scale_fwd,
        row_fwd,
        payload_bwd[0],
        lane_scale_bwd,
        row_bwd,
        cot,
        norm_gain,
        vmem=ALL_VMEM_BYTES,
    )
    sent = spread_z(packed).reshape(flight, 3, capacity, depth)
    sent = sent.transpose(1, 0, 2, 3).reshape(3 * n, depth)
    down = exchange(quarters_of([down_proj[0]]), "x")
    pair = exchange(quarters_of([gate_proj[0].T, up_proj[0].T]), "x")
    weights = regroup([jnp.concatenate([p, d], axis=0) for p, d in zip(pair, down)])
    sent, weights = barrier((sent, weights))

    weights = exchange(weights, "j")
    left, right = barrier(both_ways(sent, sent))
    far_f, far_v = both_ways(left[:n], right[n : 2 * n])
    weights, far_f, far_v, left, right = barrier((weights, far_f, far_v, left, right))

    top_c, bottom_c = both_ways(left[2 * n : 2 * n + half], right[2 * n + half :])
    pair, down = join(weights)
    far_top, far_bottom, own_f, behind_f, ahead_f = expert_call(
        functools.partial(forward_kernel, 4),
        [(far_f, n, 0), (sent, n, 0), (left, n, 0), (right, n, 0)],
        [pair, down],
        [row_block(rows) for rows in (half, half, n, n, n)],
    )
    top_c, bottom_c, far_top, far_bottom = barrier((top_c, bottom_c, far_top, far_bottom))

    back_f = both_ways(far_top, far_bottom)
    (both,) = expert_call(
        functools.partial(gate_up_kernel, 4),
        [(far_v, n, 0), (sent, n, 1), (left, n, 1), (right, n, 1)],
        [pair],
        [jax.ShapeDtypeStruct((SPLIT * n, pair.shape[0]), jnp.float32)],
    )
    back_f, both = barrier((back_f, both))

    back_f = both_ways(*with_far(ahead_f, behind_f, *back_f))
    far_top, far_bottom, own_b, behind_b, ahead_b = expert_call(
        functools.partial(backward_kernel, 5),
        [(top_c, half, 0), (bottom_c, half, 0), (sent, n, 2), (left, n, 2), (right, n, 2)],
        [both, pair, down],
        [row_block(rows) for rows in (half, half, n, n, n)],
    )
    back_f, far_top, far_bottom = barrier((back_f, far_top, far_bottom))

    mixed_fwd = spread_z(add(own_f, *back_f))
    back_b = barrier(both_ways(far_top, far_bottom))
    back_b = both_ways(*with_far(ahead_b, behind_b, *back_b))
    back_b, mixed_fwd = barrier((back_b, mixed_fwd))
    mixed_bwd = spread_z(add(own_b, *back_b))

    next_value = call(
        functools.partial(next_kernel, capacity),
        (tokens, depth),
        payload_fwd[0],
        lane_scale_fwd,
        row_fwd,
        lane_weight_fwd,
        mixed_fwd,
    )
    grad_value = call(
        functools.partial(prev_kernel, capacity),
        (tokens, depth),
        payload_bwd[0],
        lane_scale_bwd,
        norm_gain,
        row_bwd,
        lane_weight_bwd,
        cot,
        mixed_bwd,
        scratch=[pltpu.VMEM((tokens, depth), jnp.float32)],
    )
    next_rows = shifted(next_value, "section", 1)
    prev_grads = shifted(grad_value, "section", -1)
    return (next_rows[None], prev_grads[None])


def solution(mesh):
    sections, experts = mesh.devices.shape
    columns = experts // (2 * SPLIT)
    fine = Mesh(mesh.devices.reshape(sections, columns, 2, SPLIT), ("section", "x", "h", "j"))
    expert = ("x", "h", "j")
    rows = P("section", expert, None)
    return jax.shard_map(
        local,
        mesh=fine,
        in_specs=(rows,) * 9
        + (
            P("section", None),
            P("section", None, expert),
            P("section", None, expert),
            P("section", expert, None),
        ),
        out_specs=(rows, rows),
        check_vma=False,
    )
```

```python
import functools

import jax
import jax.numpy as jnp
from jax import lax
from jax.experimental import pallas as pl
from jax.experimental.pallas import tpu as pltpu
from jax.sharding import Mesh, PartitionSpec as P

SPLIT = 4
EPS = 1e-06
CONTRACT_LAST = (((1,), (1,)), ((), ()))
VMEM_BYTES = 32 * 1024 * 1024
ALL_VMEM_BYTES = 60 * 1024 * 1024
ONCE = pl.Buffered(1)
CHUNK = 512


def contract(a, b):
    return lax.dot_general(a, b, CONTRACT_LAST, preferred_element_type=jnp.float32)


def mul(a, b):
    return jnp.dot(a, b, preferred_element_type=jnp.float32)


def home_of(route):
    return lax.rem(route, 2) * SPLIT + lax.div(route, 2)


def earlier_of(route_row):
    tokens = route_row.shape[1]
    first = lax.broadcasted_iota(jnp.int32, (tokens, tokens), 0)
    second = lax.broadcasted_iota(jnp.int32, (tokens, tokens), 1)
    column = jnp.sum(jnp.where(first == second, route_row, 0), axis=1, keepdims=True)
    return column, column == route_row, first, second


def slots_in_lanes(route_row, capacity, kinds):
    _, same, above, here = earlier_of(route_row)
    earlier = jnp.where(same & (above < here), 1.0, 0.0)
    position = jnp.sum(earlier, axis=0, keepdims=True).astype(jnp.int32)
    return home_of(route_row) * (kinds * capacity) + position


def slots_in_rows(route_row, capacity):
    column, same, here, before = earlier_of(route_row)
    earlier = jnp.where(same & (before < here), 1.0, 0.0)
    position = jnp.sum(earlier, axis=1, keepdims=True).astype(jnp.int32)
    return home_of(column) * capacity + position


def as_column(row):
    tokens = row.shape[1]
    first = lax.broadcasted_iota(jnp.int32, (tokens, tokens), 0)
    second = lax.broadcasted_iota(jnp.int32, (tokens, tokens), 1)
    return jnp.sum(jnp.where(first == second, row, 0.0), axis=1, keepdims=True)


def scale_columns(scale_ref):
    blocks, _, tokens = scale_ref.shape
    rows = [scale_ref[block] for block in range(blocks)]
    rows.append(jnp.zeros((tokens - blocks, tokens), jnp.float32))
    return jnp.transpose(jnp.concatenate(rows, axis=0))


def scaled_block(payload_ref, scales, block, width):
    columns = slice(block * width, (block + 1) * width)
    return payload_ref[:, columns].astype(jnp.float32) * scales[:, block : block + 1]


def inverse_of(payload_ref, scales, blocks):
    tokens, depth = payload_ref.shape
    width = depth // blocks
    total = jnp.zeros((tokens, width), jnp.float32)
    for block in range(blocks):
        value = scaled_block(payload_ref, scales, block, width)
        total = total + value * value
    return lax.rsqrt(jnp.sum(total, axis=1, keepdims=True) * (1.0 / depth) + EPS)


def pick_slots(row_ref, capacity, kinds, kind, count):
    slots = slots_in_lanes(row_ref[...], capacity, kinds) + kind * capacity
    index = lax.broadcasted_iota(jnp.int32, (count, slots.shape[1]), 0)
    return jnp.where(index == slots, 1.0, 0.0).astype(jnp.bfloat16)


def pack_kernel(capacity, *refs):
    cot_ref, gain_ref, out_ref = refs[-3:]
    count = out_ref.shape[0]
    depth = refs[0].shape[1]
    blocks = refs[1].shape[0]
    width = depth // blocks
    sides = [(refs[at], scale_columns(refs[at + 1]), refs[at + 2]) for at in (0, 3)]
    picks = [
        pick_slots(sides[side][2], capacity, 3, kind, count)
        for side, kind in ((0, 0), (1, 1), (1, 2))
    ]
    pick = jnp.concatenate(picks, axis=1)
    inverses = [inverse_of(side[0], side[1], blocks) for side in sides]
    per_chunk = CHUNK // width
    for chunk in range(blocks // per_chunk):
        rows = []
        for side, inverse in zip(sides, inverses):
            parts = []
            for block in range(chunk * per_chunk, (chunk + 1) * per_chunk):
                columns = slice(block * width, (block + 1) * width)
                value = scaled_block(side[0], side[1], block, width)
                parts.append((value * inverse * gain_ref[:, columns]).astype(jnp.bfloat16))
            rows.append(jnp.concatenate(parts, axis=1))
        columns = slice(chunk * CHUNK, (chunk + 1) * CHUNK)
        stacked = jnp.concatenate(rows + [cot_ref[:, columns]], axis=0)
        out_ref[:, columns] = mul(pick, stacked).astype(jnp.bfloat16)


def joined(refs):
    return jnp.concatenate([ref[...] for ref in refs], axis=0)


def store_rows(out_refs, hidden, weight_ref):
    depth = weight_ref.shape[1]
    for chunk in range(depth // CHUNK):
        columns = slice(chunk * CHUNK, (chunk + 1) * CHUNK)
        value = mul(hidden, weight_ref[:, columns]).astype(jnp.bfloat16)
        start = 0
        for out_ref in out_refs:
            stop = start + out_ref.shape[0]
            out_ref[:, columns] = value[start:stop]
            start = stop


def forward_kernel(count, *refs):
    row_refs, pair_ref, down_ref, out_refs = refs[:count], refs[count], refs[count + 1], refs[count + 2 :]
    hidden_units = down_ref.shape[0]
    both = contract(joined(row_refs), pair_ref[...])
    gate_value, up_value = both[:, :hidden_units], both[:, hidden_units:]
    hidden = (gate_value / (1.0 + jnp.exp(-gate_value)) * up_value).astype(jnp.bfloat16)
    store_rows(out_refs, hidden, down_ref)


def gate_up_kernel(count, *refs):
    row_refs, pair_ref, out_ref = refs[:count], refs[count], refs[-1]
    out_ref[...] = contract(joined(row_refs), pair_ref[...])


def backward_kernel(count, *refs):
    cot_refs, both_ref, pair_ref, down_ref = refs[:count], *refs[count : count + 3]
    out_refs = refs[count + 3 :]
    hidden_units = down_ref.shape[0]
    gate_value, up_value = both_ref[:, :hidden_units], both_ref[:, hidden_units:]
    hidden_grad = contract(joined(cot_refs), down_ref[...])
    sigmoid_gate = 1.0 / (1.0 + jnp.exp(-gate_value))
    active = gate_value * sigmoid_gate
    gate_grad = hidden_grad * up_value * sigmoid_gate * (1.0 + gate_value * (1.0 - sigmoid_gate))
    up_grad = hidden_grad * active
    grads = jnp.concatenate([gate_grad, up_grad], axis=1).astype(jnp.bfloat16)
    store_rows(out_refs, grads, pair_ref)


def pick_rows(row_ref, slot_count, capacity):
    slots = slots_in_rows(row_ref[...], capacity)
    index = lax.broadcasted_iota(jnp.int32, (slots.shape[0], slot_count), 1)
    return jnp.where(index == slots, 1.0, 0.0).astype(jnp.bfloat16)


def next_kernel(capacity, payload_ref, scale_ref, row_ref, weight_ref, mixed_ref, out_ref):
    depth = payload_ref.shape[1]
    blocks = scale_ref.shape[0]
    width = depth // blocks
    scales = scale_columns(scale_ref)
    weight = as_column(weight_ref[...])
    pick = pick_rows(row_ref, mixed_ref.shape[0], capacity)
    per_chunk = CHUNK // width
    for chunk in range(blocks // per_chunk):
        columns = slice(chunk * CHUNK, (chunk + 1) * CHUNK)
        mixture = weight * mul(pick, mixed_ref[:, columns])
        value = jnp.concatenate(
            [
                scaled_block(payload_ref, scales, block, width)
                for block in range(chunk * per_chunk, (chunk + 1) * per_chunk)
            ],
            axis=1,
        )
        out_ref[:, columns] = (value + mixture).astype(jnp.bfloat16)


def prev_kernel(
    capacity,
    payload_ref,
    scale_ref,
    gain_ref,
    row_ref,
    weight_ref,
    cot_ref,
    mixed_ref,
    out_ref,
    scaled_ref,
):
    tokens, depth = payload_ref.shape
    blocks = scale_ref.shape[0]
    width = depth // blocks
    scales = scale_columns(scale_ref)
    weight = as_column(weight_ref[...])
    pick = pick_rows(row_ref, mixed_ref.shape[0], capacity)
    inverse = inverse_of(payload_ref, scales, blocks)
    total = jnp.zeros((tokens, width), jnp.float32)
    for chunk in range(depth // CHUNK):
        columns = slice(chunk * CHUNK, (chunk + 1) * CHUNK)
        grad = weight * mul(pick, mixed_ref[:, columns])
        scaled_ref[:, columns] = grad * gain_ref[:, columns]
    for block in range(blocks):
        columns = slice(block * width, (block + 1) * width)
        unit = scaled_block(payload_ref, scales, block, width) * inverse
        total = total + scaled_ref[:, columns] * unit
    mean = jnp.sum(total, axis=1, keepdims=True) * (1.0 / depth)
    for block in range(blocks):
        columns = slice(block * width, (block + 1) * width)
        unit = scaled_block(payload_ref, scales, block, width) * inverse
        grad = inverse * (scaled_ref[:, columns] - unit * mean)
        out_ref[:, columns] = (cot_ref[:, columns].astype(jnp.float32) + grad).astype(jnp.bfloat16)


def call(kernel, out, *args, scratch=(), vmem=VMEM_BYTES):
    def whole(shape):
        return pl.BlockSpec(shape, lambda i: (0,) * len(shape))

    return pl.pallas_call(
        kernel,
        grid=(1,),
        out_shape=jax.ShapeDtypeStruct(out, jnp.bfloat16),
        in_specs=[whole(arg.shape) for arg in args],
        out_specs=whole(out),
        scratch_shapes=list(scratch),
        compiler_params=pltpu.CompilerParams(vmem_limit_bytes=vmem),
    )(*args)


def expert_call(kernel, blocks, whole, outs):
    specs = [
        pl.BlockSpec((rows, array.shape[1]), lambda i, at=at: (at, 0), pipeline_mode=ONCE)
        for array, rows, at in blocks
    ] + [pl.BlockSpec(array.shape, lambda i: (0, 0), pipeline_mode=ONCE) for array in whole]
    return pl.pallas_call(
        kernel,
        grid=(1,),
        out_shape=outs,
        in_specs=specs,
        out_specs=[pl.BlockSpec(out.shape, lambda i: (0, 0), pipeline_mode=ONCE) for out in outs],
        compiler_params=pltpu.CompilerParams(vmem_limit_bytes=VMEM_BYTES),
    )(*[array for array, _, _ in blocks], *whole)


def shifted(value, axis, steps):
    count = lax.axis_size(axis)
    return lax.ppermute(value, axis, [(i, (i + steps) % count) for i in range(count)])


def by_distance(quarters, first):
    return [
        lax.dynamic_index_in_dim(quarters, lax.rem(first + steps, SPLIT), 0, keepdims=False)
        for steps in range(SPLIT)
    ]


def exchange(pieces, axis):
    return [pieces[0]] + [shifted(pieces[steps], axis, steps) for steps in range(1, SPLIT)]


def quarters_of(parts):
    quarters = [part.reshape(SPLIT, -1, part.shape[1]) for part in parts]
    whole = quarters[0] if len(quarters) == 1 else jnp.concatenate(quarters, axis=1)
    return by_distance(whole, lax.axis_index("x"))


def regroup(spread):
    by_expert = jnp.stack([spread[0], spread[3], spread[2], spread[1]])
    return by_distance(by_expert, lax.axis_index("j") - lax.axis_index("x") + SPLIT)


def join(pieces):
    rows = pieces[0].shape[0] // 3
    pair = [p[:rows] for p in pieces] + [p[rows : 2 * rows] for p in pieces]
    down = [p[2 * rows :] for p in pieces]
    return jnp.concatenate(pair, axis=0), jnp.concatenate(down, axis=0)


def spread_z(rows):
    return lax.all_to_all(rows, ("h", "j"), 0, 0, tiled=True)


def both_ways(ahead, behind):
    return shifted(ahead, "x", 1), shifted(behind, "x", -1)


def add(*terms):
    total = terms[0].astype(jnp.float32)
    for term in terms[1:]:
        total = total + term.astype(jnp.float32)
    return total.astype(jnp.bfloat16)


def with_far(ahead, behind, from_left, from_right):
    half = from_left.shape[0]
    ahead = jnp.concatenate([add(ahead[:half], from_left), ahead[half:]], axis=0)
    behind = jnp.concatenate([behind[:half], add(behind[half:], from_right)], axis=0)
    return ahead, behind


def local(
    payload_fwd,
    scale_fwd,
    routes_fwd,
    weight_fwd,
    payload_bwd,
    scale_bwd,
    routes_bwd,
    weight_bwd,
    cotangent,
    norm_gain,
    gate_proj,
    up_proj,
    down_proj,
):
    barrier = lax.optimization_barrier
    flight = 2 * SPLIT
    tokens, depth = payload_fwd.shape[1:]
    capacity = 3 * tokens // (2 * flight)
    slot_count = flight * capacity
    row_fwd, row_bwd = routes_fwd[0].reshape(1, tokens), routes_bwd[0].reshape(1, tokens)
    lane_weight_fwd = weight_fwd[0].reshape(1, tokens)
    lane_weight_bwd = weight_bwd[0].reshape(1, tokens)
    lane_scale_fwd = scale_fwd[0].T[:, None, :]
    lane_scale_bwd = scale_bwd[0].T[:, None, :]
    cot = cotangent[0]
    n, half = slot_count, slot_count // 2

    def kind_of(rows, kind):
        return rows.reshape(flight, 3, capacity, depth)[:, kind].reshape(n, depth)

    def by_kind(rows):
        apart = rows.reshape(flight, 3, capacity, depth).transpose(1, 0, 2, 3)
        return apart.reshape(3 * n, depth)

    def row_block(rows):
        return jax.ShapeDtypeStruct((rows, depth), jnp.bfloat16)

    packed = call(
        functools.partial(pack_kernel, capacity),
        (3 * n, depth),
        payload_fwd[0],
        lane_scale_fwd,
        row_fwd,
        payload_bwd[0],
        lane_scale_bwd,
        row_bwd,
        cot,
        norm_gain,
        vmem=ALL_VMEM_BYTES,
    )
    sent = spread_z(packed)
    down = exchange(quarters_of([down_proj[0]]), "x")
    pair = exchange(quarters_of([gate_proj[0].T, up_proj[0].T]), "x")
    weights = regroup([jnp.concatenate([p, d], axis=0) for p, d in zip(pair, down)])
    sent, weights = barrier((sent, weights))

    weights = exchange(weights, "j")
    left, right = barrier(both_ways(sent, sent))
    far_f, far_v = both_ways(kind_of(left, 0), kind_of(right, 1))
    weights, far_f, far_v, sent, left, right = barrier(
        (weights, far_f, far_v, by_kind(sent), by_kind(left), by_kind(right))
    )

    top_c, bottom_c = both_ways(left[2 * n : 2 * n + half], right[2 * n + half :])
    pair, down = join(weights)
    far_top, far_bottom, own_f, behind_f, ahead_f = expert_call(
        functools.partial(forward_kernel, 4),
        [(far_f, n, 0), (sent, n, 0), (left, n, 0), (right, n, 0)],
        [pair, down],
        [row_block(rows) for rows in (half, half, n, n, n)],
    )
    top_c, bottom_c, far_top, far_bottom = barrier((top_c, bottom_c, far_top, far_bottom))

    back_f = both_ways(far_top, far_bottom)
    (both,) = expert_call(
        functools.partial(gate_up_kernel, 4),
        [(far_v, n, 0), (sent, n, 1), (left, n, 1), (right, n, 1)],
        [pair],
        [jax.ShapeDtypeStruct((SPLIT * n, pair.shape[0]), jnp.float32)],
    )
    back_f, both = barrier((back_f, both))

    back_f = both_ways(*with_far(ahead_f, behind_f, *back_f))
    far_top, far_bottom, own_b, behind_b, ahead_b = expert_call(
        functools.partial(backward_kernel, 5),
        [(top_c, half, 0), (bottom_c, half, 0), (sent, n, 2), (left, n, 2), (right, n, 2)],
        [both, pair, down],
        [row_block(rows) for rows in (half, half, n, n, n)],
    )
    back_f, far_top, far_bottom = barrier((back_f, far_top, far_bottom))

    mixed_fwd = spread_z(add(own_f, *back_f))
    back_b = barrier(both_ways(far_top, far_bottom))
    back_b = both_ways(*with_far(ahead_b, behind_b, *back_b))
    back_b, mixed_fwd = barrier((back_b, mixed_fwd))
    mixed_bwd = spread_z(add(own_b, *back_b))

    next_value = call(
        functools.partial(next_kernel, capacity),
        (tokens, depth),
        payload_fwd[0],
        lane_scale_fwd,
        row_fwd,
        lane_weight_fwd,
        mixed_fwd,
    )
    grad_value = call(
        functools.partial(prev_kernel, capacity),
        (tokens, depth),
        payload_bwd[0],
        lane_scale_bwd,
        norm_gain,
        row_bwd,
        lane_weight_bwd,
        cot,
        mixed_bwd,
        scratch=[pltpu.VMEM((tokens, depth), jnp.float32)],
    )
    next_rows = shifted(next_value, "section", 1)
    prev_grads = shifted(grad_value, "section", -1)
    return (next_rows[None], prev_grads[None])


def solution(mesh):
    sections, experts = mesh.devices.shape
    columns = experts // (2 * SPLIT)
    fine = Mesh(mesh.devices.reshape(sections, columns, 2, SPLIT), ("section", "x", "h", "j"))
    expert = ("x", "h", "j")
    rows = P("section", expert, None)
    return jax.shard_map(
        local,
        mesh=fine,
        in_specs=(rows,) * 9
        + (
            P("section", None),
            P("section", None, expert),
            P("section", None, expert),
            P("section", expert, None),
        ),
        out_specs=(rows, rows),
        check_vma=False,
    )
```

```python
import functools

import jax
import jax.numpy as jnp
from jax import lax
from jax.experimental import pallas as pl
from jax.experimental.pallas import tpu as pltpu
from jax.sharding import Mesh, PartitionSpec as P

SPLIT = 4
EPS = 1e-06
CONTRACT_LAST = (((1,), (1,)), ((), ()))
VMEM_BYTES = 32 * 1024 * 1024
ALL_VMEM_BYTES = 60 * 1024 * 1024
ONCE = pl.Buffered(1)
CHUNK = 512


def contract(a, b):
    return lax.dot_general(a, b, CONTRACT_LAST, preferred_element_type=jnp.float32)


def mul(a, b):
    return jnp.dot(a, b, preferred_element_type=jnp.float32)


def home_of(route):
    return lax.rem(route, 2) * SPLIT + lax.div(route, 2)


def earlier_of(route_row):
    tokens = route_row.shape[1]
    first = lax.broadcasted_iota(jnp.int32, (tokens, tokens), 0)
    second = lax.broadcasted_iota(jnp.int32, (tokens, tokens), 1)
    column = jnp.sum(jnp.where(first == second, route_row, 0), axis=1, keepdims=True)
    return column, column == route_row, first, second


def slots_in_lanes(route_row, capacity, kinds):
    _, same, above, here = earlier_of(route_row)
    earlier = jnp.where(same & (above < here), 1.0, 0.0)
    position = jnp.sum(earlier, axis=0, keepdims=True).astype(jnp.int32)
    return home_of(route_row) * (kinds * capacity) + position


def slots_in_rows(route_row, capacity):
    column, same, here, before = earlier_of(route_row)
    earlier = jnp.where(same & (before < here), 1.0, 0.0)
    position = jnp.sum(earlier, axis=1, keepdims=True).astype(jnp.int32)
    return home_of(column) * capacity + position


def as_column(row):
    tokens = row.shape[1]
    first = lax.broadcasted_iota(jnp.int32, (tokens, tokens), 0)
    second = lax.broadcasted_iota(jnp.int32, (tokens, tokens), 1)
    return jnp.sum(jnp.where(first == second, row, 0.0), axis=1, keepdims=True)


def scale_columns(scale_ref):
    blocks, _, tokens = scale_ref.shape
    rows = [scale_ref[block] for block in range(blocks)]
    rows.append(jnp.zeros((tokens - blocks, tokens), jnp.float32))
    return jnp.transpose(jnp.concatenate(rows, axis=0))


def scaled_block(payload_ref, scales, block, width):
    columns = slice(block * width, (block + 1) * width)
    return payload_ref[:, columns].astype(jnp.float32) * scales[:, block : block + 1]


def inverse_of(payload_ref, scales, blocks):
    tokens, depth = payload_ref.shape
    width = depth // blocks
    total = jnp.zeros((tokens, width), jnp.float32)
    for block in range(blocks):
        value = scaled_block(payload_ref, scales, block, width)
        total = total + value * value
    return lax.rsqrt(jnp.sum(total, axis=1, keepdims=True) * (1.0 / depth) + EPS)


def pick_slots(row_ref, capacity, kinds, kind, count):
    slots = slots_in_lanes(row_ref[...], capacity, kinds) + kind * capacity
    index = lax.broadcasted_iota(jnp.int32, (count, slots.shape[1]), 0)
    return jnp.where(index == slots, 1.0, 0.0).astype(jnp.bfloat16)


def pack_kernel(capacity, *refs):
    cot_ref, gain_ref, out_ref = refs[-3:]
    depth = refs[0].shape[1]
    blocks = refs[1].shape[0]
    width = depth // blocks
    homes = out_ref.shape[0] // (3 * capacity)
    sides = [(refs[at], scale_columns(refs[at + 1]), refs[at + 2]) for at in (0, 3)]
    picks = [pick_slots(side[2], capacity, 1, 0, homes * capacity) for side in sides]
    inverses = [inverse_of(side[0], side[1], blocks) for side in sides]
    per_chunk = CHUNK // width
    for chunk in range(blocks // per_chunk):
        columns = slice(chunk * CHUNK, (chunk + 1) * CHUNK)
        rows = []
        for side, inverse in zip(sides, inverses):
            parts = []
            for block in range(chunk * per_chunk, (chunk + 1) * per_chunk):
                gain = gain_ref[:, block * width : (block + 1) * width]
                value = scaled_block(side[0], side[1], block, width)
                parts.append((value * inverse * gain).astype(jnp.bfloat16))
            rows.append(jnp.concatenate(parts, axis=1))
        kinds = [mul(picks[0], rows[0]), mul(picks[1], rows[1]), mul(picks[1], cot_ref[:, columns])]
        apart = [
            kind[home * capacity : (home + 1) * capacity] for home in range(homes) for kind in kinds
        ]
        out_ref[:, columns] = jnp.concatenate(apart, axis=0).astype(jnp.bfloat16)


def joined(refs):
    return jnp.concatenate([ref[...] for ref in refs], axis=0)


def store_rows(out_refs, hidden, weight_ref):
    depth = weight_ref.shape[1]
    for chunk in range(depth // CHUNK):
        columns = slice(chunk * CHUNK, (chunk + 1) * CHUNK)
        value = mul(hidden, weight_ref[:, columns]).astype(jnp.bfloat16)
        start = 0
        for out_ref in out_refs:
            stop = start + out_ref.shape[0]
            out_ref[:, columns] = value[start:stop]
            start = stop


def forward_kernel(count, *refs):
    row_refs, pair_ref, down_ref, out_refs = refs[:count], refs[count], refs[count + 1], refs[count + 2 :]
    hidden_units = down_ref.shape[0]
    both = contract(joined(row_refs), pair_ref[...])
    gate_value, up_value = both[:, :hidden_units], both[:, hidden_units:]
    hidden = (gate_value / (1.0 + jnp.exp(-gate_value)) * up_value).astype(jnp.bfloat16)
    store_rows(out_refs, hidden, down_ref)


def gate_up_kernel(count, *refs):
    row_refs, pair_ref, out_ref = refs[:count], refs[count], refs[-1]
    out_ref[...] = contract(joined(row_refs), pair_ref[...])


def backward_kernel(count, *refs):
    cot_refs, both_ref, pair_ref, down_ref = refs[:count], *refs[count : count + 3]
    out_refs = refs[count + 3 :]
    hidden_units = down_ref.shape[0]
    gate_value, up_value = both_ref[:, :hidden_units], both_ref[:, hidden_units:]
    hidden_grad = contract(joined(cot_refs), down_ref[...])
    sigmoid_gate = 1.0 / (1.0 + jnp.exp(-gate_value))
    active = gate_value * sigmoid_gate
    gate_grad = hidden_grad * up_value * sigmoid_gate * (1.0 + gate_value * (1.0 - sigmoid_gate))
    up_grad = hidden_grad * active
    grads = jnp.concatenate([gate_grad, up_grad], axis=1).astype(jnp.bfloat16)
    store_rows(out_refs, grads, pair_ref)


def pick_rows(row_ref, slot_count, capacity):
    slots = slots_in_rows(row_ref[...], capacity)
    index = lax.broadcasted_iota(jnp.int32, (slots.shape[0], slot_count), 1)
    return jnp.where(index == slots, 1.0, 0.0).astype(jnp.bfloat16)


def next_kernel(capacity, payload_ref, scale_ref, row_ref, weight_ref, mixed_ref, out_ref):
    depth = payload_ref.shape[1]
    blocks = scale_ref.shape[0]
    width = depth // blocks
    scales = scale_columns(scale_ref)
    weight = as_column(weight_ref[...])
    pick = pick_rows(row_ref, mixed_ref.shape[0], capacity)
    per_chunk = CHUNK // width
    for chunk in range(blocks // per_chunk):
        columns = slice(chunk * CHUNK, (chunk + 1) * CHUNK)
        mixture = weight * mul(pick, mixed_ref[:, columns])
        value = jnp.concatenate(
            [
                scaled_block(payload_ref, scales, block, width)
                for block in range(chunk * per_chunk, (chunk + 1) * per_chunk)
            ],
            axis=1,
        )
        out_ref[:, columns] = (value + mixture).astype(jnp.bfloat16)


def prev_kernel(
    capacity,
    payload_ref,
    scale_ref,
    gain_ref,
    row_ref,
    weight_ref,
    cot_ref,
    mixed_ref,
    out_ref,
    scaled_ref,
):
    tokens, depth = payload_ref.shape
    blocks = scale_ref.shape[0]
    width = depth // blocks
    scales = scale_columns(scale_ref)
    weight = as_column(weight_ref[...])
    pick = pick_rows(row_ref, mixed_ref.shape[0], capacity)
    inverse = inverse_of(payload_ref, scales, blocks)
    total = jnp.zeros((tokens, width), jnp.float32)
    for chunk in range(depth // CHUNK):
        columns = slice(chunk * CHUNK, (chunk + 1) * CHUNK)
        grad = weight * mul(pick, mixed_ref[:, columns])
        scaled_ref[:, columns] = grad * gain_ref[:, columns]
    for block in range(blocks):
        columns = slice(block * width, (block + 1) * width)
        unit = scaled_block(payload_ref, scales, block, width) * inverse
        total = total + scaled_ref[:, columns] * unit
    mean = jnp.sum(total, axis=1, keepdims=True) * (1.0 / depth)
    for block in range(blocks):
        columns = slice(block * width, (block + 1) * width)
        unit = scaled_block(payload_ref, scales, block, width) * inverse
        grad = inverse * (scaled_ref[:, columns] - unit * mean)
        out_ref[:, columns] = (cot_ref[:, columns].astype(jnp.float32) + grad).astype(jnp.bfloat16)


def call(kernel, out, *args, scratch=(), vmem=VMEM_BYTES):
    def whole(shape):
        return pl.BlockSpec(shape, lambda i: (0,) * len(shape))

    return pl.pallas_call(
        kernel,
        grid=(1,),
        out_shape=jax.ShapeDtypeStruct(out, jnp.bfloat16),
        in_specs=[whole(arg.shape) for arg in args],
        out_specs=whole(out),
        scratch_shapes=list(scratch),
        compiler_params=pltpu.CompilerParams(vmem_limit_bytes=vmem),
    )(*args)


def expert_call(kernel, blocks, whole, outs):
    specs = [
        pl.BlockSpec((rows, array.shape[1]), lambda i, at=at: (at, 0), pipeline_mode=ONCE)
        for array, rows, at in blocks
    ] + [pl.BlockSpec(array.shape, lambda i: (0, 0), pipeline_mode=ONCE) for array in whole]
    return pl.pallas_call(
        kernel,
        grid=(1,),
        out_shape=outs,
        in_specs=specs,
        out_specs=[pl.BlockSpec(out.shape, lambda i: (0, 0), pipeline_mode=ONCE) for out in outs],
        compiler_params=pltpu.CompilerParams(vmem_limit_bytes=VMEM_BYTES),
    )(*[array for array, _, _ in blocks], *whole)


def shifted(value, axis, steps):
    count = lax.axis_size(axis)
    return lax.ppermute(value, axis, [(i, (i + steps) % count) for i in range(count)])


def by_distance(quarters, first):
    return [
        lax.dynamic_index_in_dim(quarters, lax.rem(first + steps, SPLIT), 0, keepdims=False)
        for steps in range(SPLIT)
    ]


def exchange(pieces, axis):
    return [pieces[0]] + [shifted(pieces[steps], axis, steps) for steps in range(1, SPLIT)]


def quarters_of(parts):
    quarters = [part.reshape(SPLIT, -1, part.shape[1]) for part in parts]
    whole = quarters[0] if len(quarters) == 1 else jnp.concatenate(quarters, axis=1)
    return by_distance(whole, lax.axis_index("x"))


def regroup(spread):
    by_expert = jnp.stack([spread[0], spread[3], spread[2], spread[1]])
    return by_distance(by_expert, lax.axis_index("j") - lax.axis_index("x") + SPLIT)


def join(pieces):
    rows = pieces[0].shape[0] // 3
    pair = [p[:rows] for p in pieces] + [p[rows : 2 * rows] for p in pieces]
    down = [p[2 * rows :] for p in pieces]
    return jnp.concatenate(pair, axis=0), jnp.concatenate(down, axis=0)


def spread_z(rows):
    return lax.all_to_all(rows, ("h", "j"), 0, 0, tiled=True)


def both_ways(ahead, behind):
    return shifted(ahead, "x", 1), shifted(behind, "x", -1)


def add(*terms):
    total = terms[0].astype(jnp.float32)
    for term in terms[1:]:
        total = total + term.astype(jnp.float32)
    return total.astype(jnp.bfloat16)


def with_far(ahead, behind, from_left, from_right):
    half = from_left.shape[0]
    ahead = jnp.concatenate([add(ahead[:half], from_left), ahead[half:]], axis=0)
    behind = jnp.concatenate([behind[:half], add(behind[half:], from_right)], axis=0)
    return ahead, behind


def local(
    payload_fwd,
    scale_fwd,
    routes_fwd,
    weight_fwd,
    payload_bwd,
    scale_bwd,
    routes_bwd,
    weight_bwd,
    cotangent,
    norm_gain,
    gate_proj,
    up_proj,
    down_proj,
):
    barrier = lax.optimization_barrier
    flight = 2 * SPLIT
    tokens, depth = payload_fwd.shape[1:]
    capacity = 3 * tokens // (2 * flight)
    slot_count = flight * capacity
    row_fwd, row_bwd = routes_fwd[0].reshape(1, tokens), routes_bwd[0].reshape(1, tokens)
    lane_weight_fwd = weight_fwd[0].reshape(1, tokens)
    lane_weight_bwd = weight_bwd[0].reshape(1, tokens)
    lane_scale_fwd = scale_fwd[0].T[:, None, :]
    lane_scale_bwd = scale_bwd[0].T[:, None, :]
    cot = cotangent[0]
    n, half = slot_count, slot_count // 2

    def kind_of(rows, kind):
        return rows.reshape(flight, 3, capacity, depth)[:, kind].reshape(n, depth)

    def by_kind(rows):
        apart = rows.reshape(flight, 3, capacity, depth).transpose(1, 0, 2, 3)
        return apart.reshape(3 * n, depth)

    def row_block(rows):
        return jax.ShapeDtypeStruct((rows, depth), jnp.bfloat16)

    packed = call(
        functools.partial(pack_kernel, capacity),
        (3 * n, depth),
        payload_fwd[0],
        lane_scale_fwd,
        row_fwd,
        payload_bwd[0],
        lane_scale_bwd,
        row_bwd,
        cot,
        norm_gain,
        vmem=ALL_VMEM_BYTES,
    )
    sent = spread_z(packed)
    down = exchange(quarters_of([down_proj[0]]), "x")
    pair = exchange(quarters_of([gate_proj[0].T, up_proj[0].T]), "x")
    weights = regroup([jnp.concatenate([p, d], axis=0) for p, d in zip(pair, down)])
    sent, weights = barrier((sent, weights))

    weights = exchange(weights, "j")
    left, right = barrier(both_ways(sent, sent))
    far_f, far_v = both_ways(kind_of(left, 0), kind_of(right, 1))
    weights, far_f, far_v, sent, left, right = barrier(
        (weights, far_f, far_v, by_kind(sent), by_kind(left), by_kind(right))
    )

    top_c, bottom_c = both_ways(left[2 * n : 2 * n + half], right[2 * n + half :])
    pair, down = join(weights)
    far_top, far_bottom, own_f, behind_f, ahead_f = expert_call(
        functools.partial(forward_kernel, 4),
        [(far_f, n, 0), (sent, n, 0), (left, n, 0), (right, n, 0)],
        [pair, down],
        [row_block(rows) for rows in (half, half, n, n, n)],
    )
    top_c, bottom_c, far_top, far_bottom = barrier((top_c, bottom_c, far_top, far_bottom))

    back_f = both_ways(far_top, far_bottom)
    (both,) = expert_call(
        functools.partial(gate_up_kernel, 4),
        [(far_v, n, 0), (sent, n, 1), (left, n, 1), (right, n, 1)],
        [pair],
        [jax.ShapeDtypeStruct((SPLIT * n, pair.shape[0]), jnp.float32)],
    )
    back_f, both = barrier((back_f, both))

    back_f = both_ways(*with_far(ahead_f, behind_f, *back_f))
    far_top, far_bottom, own_b, behind_b, ahead_b = expert_call(
        functools.partial(backward_kernel, 5),
        [(top_c, half, 0), (bottom_c, half, 0), (sent, n, 2), (left, n, 2), (right, n, 2)],
        [both, pair, down],
        [row_block(rows) for rows in (half, half, n, n, n)],
    )
    back_f, far_top, far_bottom = barrier((back_f, far_top, far_bottom))

    mixed_fwd = spread_z(add(own_f, *back_f))
    back_b = barrier(both_ways(far_top, far_bottom))
    back_b = both_ways(*with_far(ahead_b, behind_b, *back_b))
    back_b, mixed_fwd = barrier((back_b, mixed_fwd))
    mixed_bwd = spread_z(add(own_b, *back_b))

    next_value = call(
        functools.partial(next_kernel, capacity),
        (tokens, depth),
        payload_fwd[0],
        lane_scale_fwd,
        row_fwd,
        lane_weight_fwd,
        mixed_fwd,
    )
    next_rows = shifted(next_value, "section", 1)
    next_rows, mixed_bwd = barrier((next_rows, mixed_bwd))
    grad_value = call(
        functools.partial(prev_kernel, capacity),
        (tokens, depth),
        payload_bwd[0],
        lane_scale_bwd,
        norm_gain,
        row_bwd,
        lane_weight_bwd,
        cot,
        mixed_bwd,
        scratch=[pltpu.VMEM((tokens, depth), jnp.float32)],
    )
    prev_grads = shifted(grad_value, "section", -1)
    return (next_rows[None], prev_grads[None])


def solution(mesh):
    sections, experts = mesh.devices.shape
    columns = experts // (2 * SPLIT)
    fine = Mesh(mesh.devices.reshape(sections, columns, 2, SPLIT), ("section", "x", "h", "j"))
    expert = ("x", "h", "j")
    rows = P("section", expert, None)
    return jax.shard_map(
        local,
        mesh=fine,
        in_specs=(rows,) * 9
        + (
            P("section", None),
            P("section", None, expert),
            P("section", None, expert),
            P("section", expert, None),
        ),
        out_specs=(rows, rows),
        check_vma=False,
    )
```
